32 devices in a mesh: ctx: 8 (over z, y), tp: 4 (over x, core).
Axes of the slice: x: 2, y: 2, z: 4, core: 2. Of those that a mesh axis runs over, the one named last changes fastest.
Arguments:
- queries: bfloat16 [1024, 32, 128], P('ctx', 'tp'), may hold values from -25 to 25
- key_vectors: bfloat16 [1024, 4, 128], P('ctx', 'tp'), may hold values from -6 to 6
- value_vectors: bfloat16 [1024, 4, 128], P('ctx', 'tp'), may hold values from -6 to 6
- attention_out: bfloat16 [1024, 32, 128], P('ctx', 'tp'), may hold values from -6 to 6
- grad_attention: bfloat16 [1024, 32, 128], P('ctx', 'tp'), may hold values from -6 to 6
- mix_input: bfloat16 [1024, 8192], P('ctx', 'tp'), may hold values from -0.125 to 0.125
- grad_mix: bfloat16 [1024, 8192], P('ctx', 'tp'), may hold values from -6 to 6
- input_map: float32 [1024, 16], P('ctx'), may hold values from -0.625 to 0.625
- output_map: float32 [1024, 16], P('ctx'), may hold values from -0.625 to 0.625
- decay_log: float32 [1024, 128], P('ctx', 'tp'), may hold values from -0.6 to 0
Outputs:
- grad_queries: bfloat16 [1024, 32, 128], P('ctx', 'tp')
- grad_keys: bfloat16 [1024, 4, 128], P('ctx', 'tp')
- grad_values: bfloat16 [1024, 4, 128], P('ctx', 'tp')
- grad_input: bfloat16 [1024, 8192], P('ctx', 'tp')
- grad_input_map: float32 [1024, 16], P('ctx')
- grad_output_map: float32 [1024, 16], P('ctx')
- grad_decay: float32 [1024, 128], P('ctx', 'tp')
The draws below stay inside these ranges and needn't reach their ends.
All inputs are finite; a program needn't handle non-finite values.
Results may differ from the reference program's by a relative error of at most 0.0052.
Values may be sent and summed in bfloat16 or wider, within the bound.
A program may use at most 128 MiB of HBM per device.

```python
import math
import jax
import jax.numpy as jnp
from jax import lax

H = 32
G = 4
HD = 128
MC = 8192
N = 16
TOK_DEV = 128
SEQUENCE_TOKENS = 1024
DECAY_GROUPS = 128


def pair_draws(key):
    folded = jax.random.fold_in(key, 11)
    random_seeds = jax.random.split(folded, 2)
    keys_raw = jnp.clip(jax.random.normal(random_seeds[0], (SEQUENCE_TOKENS, G, HD), jnp.float32), -6.0, 6.0)
    query_raw = jnp.clip(jax.random.normal(random_seeds[1], (SEQUENCE_TOKENS, H, HD), jnp.float32), -6.0, 6.0)
    return (query_raw, keys_raw)


def draw_queries(key, part):
    return pair_draws(key)[0].astype(jnp.bfloat16)


def draw_key_vectors(key, part):
    return pair_draws(key)[1].astype(jnp.bfloat16)


def draw_decay_log(key, part):
    folded = jax.random.fold_in(key, 29)
    random_seeds = jax.random.split(folded, 7)
    fast_share = 0.5
    fast_heads = jax.random.bernoulli(random_seeds[0], fast_share, (DECAY_GROUPS,))
    fast_rate = jnp.exp(jax.random.uniform(random_seeds[1], (DECAY_GROUPS,), jnp.float32, math.log(1.0 / 50.0), math.log(1.0 / 30.0)))
    slow_rate = jnp.exp(jax.random.uniform(random_seeds[2], (DECAY_GROUPS,), jnp.float32, math.log(0.2 / SEQUENCE_TOKENS), math.log(0.8 / SEQUENCE_TOKENS)))
    rates = jnp.where(fast_heads, fast_rate, slow_rate)
    device_factor = jnp.exp(jax.random.uniform(random_seeds[3], (SEQUENCE_TOKENS // TOK_DEV, DECAY_GROUPS), jnp.float32, -0.35, 0.35))
    device_factor = jnp.repeat(device_factor, TOK_DEV, axis=0)
    roughness = jax.random.uniform(random_seeds[4], (SEQUENCE_TOKENS, DECAY_GROUPS), jnp.float32, 0.5, 1.5)
    decay_factors = -rates[None, :] * device_factor * roughness
    spike_position = jax.random.randint(random_seeds[5], (2,), 0, SEQUENCE_TOKENS)
    spike_loss = jax.random.uniform(random_seeds[6], (2, DECAY_GROUPS), jnp.float32, 0.2, 0.4)
    token_positions = jnp.arange(SEQUENCE_TOKENS)
    decay_factors = decay_factors + jnp.where(token_positions[:, None] == spike_position[0], jnp.log(1.0 - spike_loss[0])[None, :], 0.0)
    decay_factors = decay_factors + jnp.where(token_positions[:, None] == spike_position[1], jnp.log(1.0 - spike_loss[1])[None, :], 0.0)
    return decay_factors


def steps_of(stream_key, extent, pieces, smallest, high):
    gain, own = 1.0, jax.random.fold_in(stream_key, 6)
    for axis_at, blocks in pieces:
        heights = jnp.exp(jax.random.uniform(jax.random.fold_in(own, axis_at), (blocks,), jnp.float32, smallest / len(pieces), high / len(pieces)))
        gain = gain * jnp.repeat(heights, extent[axis_at] // blocks).reshape([-1 if axis == axis_at else 1 for axis in range(len(extent))])
    return gain


def gaussian(stream_key, extent, deviation, bound, pieces=(), kind=jnp.bfloat16):
    array = deviation * jax.random.normal(stream_key, extent, jnp.float32)
    if pieces:
        array = array * steps_of(stream_key, extent, pieces, -0.22, 0.18)
    return jnp.clip(array, -bound, bound).astype(kind)


def setup_inputs(seed: int = 0) -> dict:
    keys = jax.random.split(jax.random.key(seed), 11)
    return {
        "queries": draw_queries(jax.random.fold_in(keys[10], 71), 0),
        "key_vectors": draw_key_vectors(jax.random.fold_in(keys[10], 71), 0),
        "value_vectors": gaussian(keys[2], (SEQUENCE_TOKENS, G, HD), 1.0, 6.0, ((0, 8), (1, 4))),
        "attention_out": gaussian(keys[3], (SEQUENCE_TOKENS, H, HD), 1.0, 6.0, ((0, 8), (1, 4))),
        "grad_attention": gaussian(keys[4], (SEQUENCE_TOKENS, H, HD), 1.0, 6.0, ((0, 8), (1, 4))),
        "mix_input": gaussian(keys[5], (SEQUENCE_TOKENS, MC), (4.0 / (MC ** 0.5 * SEQUENCE_TOKENS ** 0.25)), 0.125, ((0, 8), (1, 4))),
        "grad_mix": gaussian(keys[6], (SEQUENCE_TOKENS, MC), 1.0, 6.0, ((0, 8), (1, 4))),
        "input_map": gaussian(keys[7], (SEQUENCE_TOKENS, N), (1.0 / (N ** 0.5 * SEQUENCE_TOKENS ** 0.25)), 0.625, ((0, 8),), jnp.float32),
        "output_map": gaussian(keys[8], (SEQUENCE_TOKENS, N), (1.0 / (N ** 0.5 * SEQUENCE_TOKENS ** 0.25)), 0.625, ((0, 8),), jnp.float32),
        "decay_log": draw_decay_log(jax.random.fold_in(keys[10], 71), 0),
    }


def attention_part(queries, key_vectors, value_vectors, attention_out, grad_attention):
    all_tokens, head_count, head_width = queries.shape
    group_count = key_vectors.shape[1]
    repeats = head_count // group_count
    score_scale = 1.0 / math.sqrt(head_width)
    highest = lax.Precision.HIGHEST
    row_block = math.gcd(all_tokens, 256)
    key_all = key_vectors.astype(jnp.float32)
    value_all = value_vectors.astype(jnp.float32)
    grad_key_acc = jnp.zeros((all_tokens, group_count, head_width), jnp.float32)
    grad_value_acc = jnp.zeros((all_tokens, group_count, head_width), jnp.float32)
    query_pieces = []
    for block_index in range(all_tokens // row_block):
        first_row = block_index * row_block
        end_row = first_row + row_block
        query_part = queries[first_row:end_row].astype(jnp.float32).reshape(row_block, group_count, repeats, head_width)
        grad_part = grad_attention[first_row:end_row].astype(jnp.float32).reshape(row_block, group_count, repeats, head_width)
        out_part = attention_out[first_row:end_row].astype(jnp.float32).reshape(row_block, group_count, repeats, head_width)
        key_part = key_all[:end_row]
        value_part = value_all[:end_row]
        scores = jnp.einsum('tgrd,kgd->gtrk', query_part, key_part, precision=highest) * score_scale
        allowed = jnp.arange(end_row)[None, :] <= (first_row + jnp.arange(row_block))[:, None]
        scores = jnp.where(allowed[None, :, None, :], scores, -jnp.inf)
        top_score = lax.optimization_barrier(jnp.max(scores, axis=-1, keepdims=True))
        log_total = top_score + jnp.log(lax.optimization_barrier(jnp.sum(jnp.exp(scores - top_score), axis=-1, keepdims=True)))
        probs = jnp.exp(scores - log_total)
        probs_low = lax.optimization_barrier(probs.astype(jnp.bfloat16)).astype(jnp.float32)
        out_dots = lax.optimization_barrier(jnp.sum(grad_part * out_part, axis=-1)).transpose(1, 0, 2)
        grad_probs = jnp.einsum('tgrd,kgd->gtrk', grad_part, value_part, precision=highest)
        grad_scores = (probs * (grad_probs - out_dots[..., None]) * score_scale).astype(jnp.bfloat16)
        grad_scores = lax.optimization_barrier(grad_scores).astype(jnp.float32)
        query_grad = jnp.einsum('gtrk,kgd->tgrd', grad_scores, key_part, precision=highest)
        query_pieces.append(query_grad.reshape(row_block, head_count, head_width))
        grad_key_acc = grad_key_acc.at[:end_row].add(jnp.einsum('gtrk,tgrd->kgd', grad_scores, query_part, precision=highest))
        grad_value_acc = grad_value_acc.at[:end_row].add(jnp.einsum('gtrk,tgrd->kgd', probs_low, grad_part, precision=highest))
    grad_queries = jnp.concatenate(query_pieces, axis=0).astype(jnp.bfloat16)
    return (grad_queries, grad_key_acc.astype(jnp.bfloat16), grad_value_acc.astype(jnp.bfloat16))

def mixer_forward(mix_values, input_map, output_map, decay_log):
    all_tokens, channels = mix_values.shape
    group_count = decay_log.shape[1]
    group_width = channels // group_count
    state_size = input_map.shape[1]
    step_len = math.gcd(all_tokens, 128)
    block_count = all_tokens // step_len

    def token_step(state, inputs):
        token_in, in_map, out_map, token_log = inputs
        state = jnp.exp(token_log)[:, None, None] * state + token_in[:, :, None] * in_map[None, None, :]
        return (state, jnp.einsum('hpn,n->hp', state, out_map, precision=lax.Precision.HIGHEST))

    def block_step(state, inputs):
        return lax.scan(token_step, state, inputs)
    inputs = (mix_values.reshape(block_count, step_len, group_count, group_width), input_map.reshape(block_count, step_len, state_size), output_map.reshape(block_count, step_len, state_size), decay_log.reshape(block_count, step_len, group_count))
    initial = jnp.zeros((group_count, group_width, state_size), jnp.float32)
    final_state, outputs = lax.scan(jax.checkpoint(block_step), initial, inputs)
    return outputs.reshape(all_tokens, channels)

def reference(queries, key_vectors, value_vectors, attention_out, grad_attention, mix_input, grad_mix, input_map, output_map, decay_log):
    grad_queries, grad_keys, grad_values = attention_part(queries, key_vectors, value_vectors, attention_out, grad_attention)
    scan_out, pullback = jax.vjp(mixer_forward, mix_input.astype(jnp.float32), input_map, output_map, decay_log)
    grad_mix_in, grad_in_map, grad_out_map, grad_decay = pullback(grad_mix.astype(jnp.float32))
    return (grad_queries, grad_keys, grad_values, grad_mix_in.astype(jnp.bfloat16), grad_in_map, grad_out_map, grad_decay)
```

```python
import functools
import math

import jax
import jax.numpy as jnp
from jax import lax
from jax.experimental import pallas as pl
from jax.experimental.pallas import tpu as pltpu
from jax.sharding import PartitionSpec as P

F32 = jnp.float32
BF16 = jnp.bfloat16
MESH = pl.DeviceIdType.MESH
LOG2E = math.log2(math.e)
MASKED = -1e30


def mm(a, b):
    return lax.dot_general(a, b, (((1,), (0,)), ((), ())), preferred_element_type=F32)


def mm_nt(a, b):
    return lax.dot_general(a, b, (((1,), (1,)), ((), ())), preferred_element_type=F32)


def mm_full(a, b):
    return lax.dot_general(
        a, b, (((1,), (0,)), ((), ())), precision=lax.Precision.HIGHEST, preferred_element_type=F32
    )


def halves(a):
    high = a.astype(BF16)
    return high, (a - high.astype(F32)).astype(BF16)


def mm_split(a, b):
    high, low = halves(a)
    return mm(high, b) + mm(low, b)


def mm_nt_split(a, b):
    high, low = halves(a)
    return mm_nt(high, b) + mm_nt(low, b)


def kernel(
    n,
    ntp,
    heads,
    q_ref,
    k_ref,
    v_ref,
    o_ref,
    go_ref,
    x_ref,
    g_ref,
    bm_ref,
    cm_ref,
    dl_ref,
    gq_ref,
    gk_ref,
    gv_ref,
    gx_ref,
    gb_ref,
    gc_ref,
    gd_ref,
    kv,
    st,
    st_out,
    tot,
    grad_out,
    grad_in,
    tp_buf,
    gs,
    xs,
    ends_pre,
    e_wide,
    f_wide,
    half_wide,
    dots_row,
    stat_max,
    stat_sum,
    gq_t,
    kv_s,
    kv_r,
    st_s,
    st_r,
    tt_s,
    tt_r,
    gr_s,
    gr_r,
    tp_s,
    tp_r,
):
    me = lax.axis_index("ctx")
    me_tp = lax.axis_index("tp")
    tokens, channels = x_ref.shape
    groups = dl_ref.shape[1]
    state = bm_ref.shape[1]
    rows, width = q_ref.shape
    chunk = 256
    score_scale = 1.0 / math.sqrt(width)

    barrier = pltpu.get_barrier_semaphore()

    def greet_ctx(d, c):
        pl.semaphore_signal(
            barrier, inc=1, device_id={"ctx": lax.rem(me + d, n)}, device_id_type=MESH
        )
        return c

    def greet_tp(d, c):
        pl.semaphore_signal(
            barrier, inc=1, device_id={"tp": lax.rem(me_tp + d, ntp)}, device_id_type=MESH
        )
        return c

    lax.fori_loop(1, n, greet_ctx, 0)
    lax.fori_loop(1, ntp, greet_tp, 0)
    kv[me, 0:tokens, :] = k_ref[...]
    kv[me, tokens : 2 * tokens, :] = v_ref[...]
    pl.semaphore_wait(barrier, n - 1 + ntp - 1)

    def kv_copy(src, dst):
        return pltpu.make_async_remote_copy(
            src_ref=kv.at[src],
            dst_ref=kv.at[src],
            send_sem=kv_s.at[dst],
            recv_sem=kv_r.at[src],
            device_id={"ctx": dst},
            device_id_type=MESH,
        )

    def state_copy(src, dst, which):
        return pltpu.make_async_remote_copy(
            src_ref=st_out.at[which],
            dst_ref=st.at[src],
            send_sem=st_s.at[dst],
            recv_sem=st_r.at[src],
            device_id={"ctx": dst},
            device_id_type=MESH,
        )

    def tot_copy(src, dst):
        return pltpu.make_async_remote_copy(
            src_ref=tot.at[src],
            dst_ref=tot.at[src],
            send_sem=tt_s.at[dst],
            recv_sem=tt_r.at[src],
            device_id={"ctx": dst},
            device_id_type=MESH,
        )

    def grad_copy(src, dst):
        return pltpu.make_async_remote_copy(
            src_ref=grad_out.at[dst],
            dst_ref=grad_in.at[src],
            send_sem=gr_s.at[dst],
            recv_sem=gr_r.at[src],
            device_id={"ctx": dst},
            device_id_type=MESH,
        )

    def tp_copy(src, dst):
        return pltpu.make_async_remote_copy(
            src_ref=tp_buf.at[src],
            dst_ref=tp_buf.at[src],
            send_sem=tp_s.at[dst],
            recv_sem=tp_r.at[src],
            device_id={"tp": dst},
            device_id_type=MESH,
        )

    def send_kv(dst, c):
        kv_copy(me, dst).start()
        return c

    lax.fori_loop(me + 1, n, send_kv, 0)

    token_row = lax.broadcasted_iota(jnp.int32, (tokens, tokens), 0)
    token_col = lax.broadcasted_iota(jnp.int32, (tokens, tokens), 1)
    lower = token_row >= token_col
    seg = (
        lax.broadcasted_iota(jnp.int32, (groups, channels), 1) // (channels // groups)
        == lax.broadcasted_iota(jnp.int32, (groups, channels), 0)
    ).astype(F32).astype(BF16)
    cum = mm_full(lower.astype(F32), dl_ref[...])
    total = cum[tokens - 1 : tokens, :]
    mid = 0.5 * total
    e_wide[...] = mm_split(jnp.exp(cum - mid), seg)
    f_wide[...] = mm_split(jnp.exp(mid - cum), seg)
    half_wide[...] = mm_split(jnp.exp(jnp.broadcast_to(mid, (state, groups))), seg)
    gs[0:tokens, :] = (e_wide[...] * g_ref[...].astype(F32)).astype(BF16)
    xs[0:tokens, :] = (f_wide[...] * x_ref[...].astype(F32)).astype(BF16)
    in_map = bm_ref[...]
    out_map = cm_ref[...]
    maps_t = jnp.concatenate(
        [in_map, out_map, jnp.zeros((tokens, 128 - 2 * state), F32)], axis=1
    ).T
    in_map_t = maps_t[0:state, :]
    out_map_t = maps_t[state : 2 * state, :]
    ends_pre[...] = mm_split(in_map_t, xs[0:tokens, :])
    st_out[0] = (half_wide[...] * ends_pre[...]).astype(BF16)
    st_out[1] = (half_wide[...] * mm_split(out_map_t, gs[0:tokens, :])).astype(BF16)
    tot[me] = jnp.broadcast_to(
        jnp.concatenate([total, jnp.zeros((1, 128 - groups), F32)], axis=1), (8, 128)
    )

    def send_states(d, c):
        dst = lax.rem(me + d, n)
        tot_copy(me, dst).start()

        @pl.when(dst > me)
        def _():
            state_copy(me, dst, 0).start()

        @pl.when(dst < me)
        def _():
            state_copy(me, dst, 1).start()

        return c

    lax.fori_loop(1, n, send_states, 0)

    key_at = lax.broadcasted_iota(jnp.int32, (tokens, chunk), 0)
    pair_at = lax.broadcasted_iota(jnp.int32, (tokens, chunk), 1)
    ones_row = jnp.ones((8, width), BF16)

    for first in range(0, rows, chunk):
        part = pl.ds(first, chunk)
        prod = go_ref[part, :].astype(F32) * o_ref[part, :].astype(F32)
        high, low = halves(prod)
        dots_row[:, part] = mm_nt(ones_row, high) + mm_nt(ones_row, low)

    def scores_of(keys, first, diagonal):
        scores = mm_nt(keys, q_ref[pl.ds(first, chunk), :]) * (score_scale * LOG2E)
        if diagonal:
            scores = jnp.where(key_at <= (pair_at + first) // heads, scores, MASKED)
        return scores

    own_keys = k_ref[...]
    for first in range(0, rows, chunk):
        part = pl.ds(first, chunk)
        scores = scores_of(own_keys, first, True)
        top = jnp.max(scores, axis=0, keepdims=True)
        stat_max[:, part] = jnp.broadcast_to(top, (8, chunk))
        stat_sum[:, part] = jnp.broadcast_to(
            jnp.sum(jnp.exp2(scores - top), axis=0, keepdims=True), (8, chunk)
        )

    def stats_step(d, c):
        src = me - d
        kv_copy(src, me).wait_recv()
        keys = kv[src, 0:tokens, :]
        for first in range(0, rows, chunk):
            part = pl.ds(first, chunk)
            scores = scores_of(keys, first, False)
            before = stat_max[0:1, part]
            top = jnp.maximum(before, jnp.max(scores, axis=0, keepdims=True))
            summed = stat_sum[0:1, part] * jnp.exp2(before - top) + jnp.sum(
                jnp.exp2(scores - top), axis=0, keepdims=True
            )
            stat_max[:, part] = jnp.broadcast_to(top, (8, chunk))
            stat_sum[:, part] = jnp.broadcast_to(summed, (8, chunk))
        return c

    lax.fori_loop(1, me + 1, stats_step, 0)
    stat_max[...] = stat_max[...] + jnp.log(stat_sum[...]) * LOG2E
    gq_t[...] = jnp.zeros_like(gq_t)

    def grads_of(keys, values, diagonal):
        keys_t = keys.astype(F32).T.astype(BF16)
        key_sum = jnp.zeros((tokens, width), F32)
        value_sum = jnp.zeros((tokens, width), F32)
        for first in range(0, rows, chunk):
            part = pl.ds(first, chunk)
            queries = q_ref[part, :]
            grads = go_ref[part, :]
            probs = jnp.exp2(scores_of(keys, first, diagonal) - stat_max[0:1, part])
            grad_probs = mm_nt(values, grads)
            grad_scores = (probs * (grad_probs - dots_row[0:1, part]) * score_scale).astype(BF16)
            value_sum = value_sum + mm(probs.astype(BF16), grads)
            key_sum = key_sum + mm(grad_scores, queries)
            gq_t[:, part] += mm(keys_t, grad_scores)
        return key_sum, value_sum

    def grads_step(src, c):
        key_sum, value_sum = grads_of(kv[src, 0:tokens, :], kv[src, tokens : 2 * tokens, :], False)
        grad_out[src, 0:tokens, :] = key_sum.astype(BF16)
        grad_out[src, tokens : 2 * tokens, :] = value_sum.astype(BF16)
        grad_copy(me, src).start()
        return c

    lax.fori_loop(0, me, grads_step, 0)
    own_key_sum, own_value_sum = grads_of(own_keys, v_ref[...], True)
    gq_ref[...] = gq_t[...].T.astype(BF16)

    def take_states(start, src_of):
        def step(d, carry):
            summed, log_sum = carry
            src = src_of(d)
            tot_copy(src, me).wait_recv()
            state_copy(src, me, 0).wait_recv()
            summed = summed + mm_split(jnp.exp(log_sum), seg) * st[src].astype(F32)
            log_sum = log_sum + jnp.broadcast_to(tot[src][0:1, 0:groups], (state, groups))
            return summed, log_sum

        zero = (jnp.zeros((state, channels), F32), jnp.zeros((state, groups), F32))
        return lax.fori_loop(1, start, step, zero)[0]

    state_in = take_states(me + 1, lambda d: me - d) * half_wide[...]
    pull_in = take_states(n - me, lambda d: me + d) * half_wide[...]
    xs[tokens : tokens + state, :] = state_in.astype(BF16)
    gs[tokens : tokens + state, :] = pull_in.astype(BF16)
    kernel_sum = jnp.where(lower, mm_nt(gs[0:tokens, :], xs[0:tokens, :]), 0.0)
    tp_buf[me_tp, 0:state, :] = mm_full(out_map_t, kernel_sum) + mm_nt(
        gs[tokens : tokens + state, :], xs[0:tokens, :]
    )
    tp_buf[me_tp, state : 2 * state, :] = mm_full(in_map_t, kernel_sum.T) + mm_nt(
        xs[tokens : tokens + state, :], gs[0:tokens, :]
    )

    def send_tp(d, c):
        tp_copy(me_tp, lax.rem(me_tp + d, ntp)).start()
        return c

    lax.fori_loop(1, ntp, send_tp, 0)

    map_dots = jnp.where(lower, mm_full(out_map, in_map_t), 0.0)
    forward = jnp.concatenate([map_dots.astype(BF16), out_map.astype(BF16)], axis=1)
    backward = jnp.concatenate([map_dots.T.astype(BF16), in_map.astype(BF16)], axis=1)
    out_pre = mm(forward, xs[...])
    in_pre = mm(backward, gs[...])
    gx_ref[...] = (f_wide[...] * in_pre).astype(BF16)
    per_token = gs[0:tokens, :].astype(F32) * out_pre - xs[0:tokens, :].astype(F32) * in_pre
    at_end = pull_in * (state_in + ends_pre[...])
    seg_token = mm_nt_split(per_token, seg)
    seg_end = mm_nt_split(at_end, seg)
    gd_ref[...] = mm_full((token_row <= token_col).astype(F32), seg_token) + jnp.sum(
        seg_end, axis=0, keepdims=True
    )

    def take_grads(src, carry):
        grad_copy(src, me).wait_recv()
        return (
            carry[0] + grad_in[src, 0:tokens, :].astype(F32),
            carry[1] + grad_in[src, tokens : 2 * tokens, :].astype(F32),
        )

    key_total, value_total = lax.fori_loop(
        me + 1, n, take_grads, (own_key_sum, own_value_sum)
    )
    gk_ref[...] = key_total.astype(BF16)
    gv_ref[...] = value_total.astype(BF16)

    def wait_tp(d, c):
        tp_copy(lax.rem(me_tp + d, ntp), me_tp).wait_recv()
        return c

    lax.fori_loop(1, ntp, wait_tp, 0)
    map_grads = tp_buf[0]
    for other in range(1, ntp):
        map_grads = map_grads + tp_buf[other]
    map_grads = jnp.concatenate([map_grads, jnp.zeros((128 - 2 * state, tokens), F32)], axis=0).T
    gb_ref[...] = map_grads[:, 0:state]
    gc_ref[...] = map_grads[:, state : 2 * state]

    def end_tp(d, c):
        tp_copy(me_tp, lax.rem(me_tp + d, ntp)).wait_send()
        return c

    def end_states(d, c):
        dst = lax.rem(me + d, n)
        tot_copy(me, dst).wait_send()
        state_copy(me, dst, 0).wait_send()
        return c

    def end_kv(dst, c):
        kv_copy(me, dst).wait_send()
        return c

    def end_grads(dst, c):
        grad_copy(me, dst).wait_send()
        return c

    lax.fori_loop(1, ntp, end_tp, 0)
    lax.fori_loop(1, n, end_states, 0)
    lax.fori_loop(me + 1, n, end_kv, 0)
    lax.fori_loop(0, me, end_grads, 0)


def local(
    n,
    ntp,
    queries,
    key_vectors,
    value_vectors,
    attention_out,
    grad_attention,
    mix_input,
    grad_mix,
    input_map,
    output_map,
    decay_log,
):
    tokens, heads, width = queries.shape
    channels = mix_input.shape[1]
    state = input_map.shape[1]
    groups = decay_log.shape[1]
    rows = tokens * heads
    flat = lambda a: a.reshape(-1, width)
    vmem = pl.BlockSpec(memory_space=pltpu.VMEM)
    dma = pltpu.SemaphoreType.DMA
    outs = pl.pallas_call(
        functools.partial(kernel, n, ntp, heads),
        out_shape=(
            jax.ShapeDtypeStruct((rows, width), BF16),
            jax.ShapeDtypeStruct((tokens, width), BF16),
            jax.ShapeDtypeStruct((tokens, width), BF16),
            jax.ShapeDtypeStruct((tokens, channels), BF16),
            jax.ShapeDtypeStruct((tokens, state), F32),
            jax.ShapeDtypeStruct((tokens, state), F32),
            jax.ShapeDtypeStruct((tokens, groups), F32),
        ),
        in_specs=[vmem] * 10,
        out_specs=(vmem,) * 7,
        scratch_shapes=[
            pltpu.VMEM((n, 2 * tokens, width), BF16),
            pltpu.VMEM((n, state, channels), BF16),
            pltpu.VMEM((2, state, channels), BF16),
            pltpu.VMEM((n, 8, 128), F32),
            pltpu.VMEM((n, 2 * tokens, width), BF16),
            pltpu.VMEM((n, 2 * tokens, width), BF16),
            pltpu.VMEM((ntp, 2 * state, tokens), F32),
            pltpu.VMEM((tokens + state, channels), BF16),
            pltpu.VMEM((tokens + state, channels), BF16),
            pltpu.VMEM((state, channels), F32),
            pltpu.VMEM((tokens, channels), F32),
            pltpu.VMEM((tokens, channels), F32),
            pltpu.VMEM((state, channels), F32),
            pltpu.VMEM((8, rows), F32),
            pltpu.VMEM((8, rows), F32),
            pltpu.VMEM((8, rows), F32),
            pltpu.VMEM((width, rows), F32),
            dma((n,)),
            dma((n,)),
            dma((n,)),
            dma((n,)),
            dma((n,)),
            dma((n,)),
            dma((n,)),
            dma((n,)),
            dma((ntp,)),
            dma((ntp,)),
        ],
        compiler_params=pltpu.CompilerParams(
            collective_id=0, has_side_effects=True, vmem_limit_bytes=48 * 1024 * 1024
        ),
        name="layer_grads",
    )(
        flat(queries),
        flat(key_vectors),
        flat(value_vectors),
        flat(attention_out),
        flat(grad_attention),
        mix_input,
        grad_mix,
        input_map,
        output_map,
        decay_log,
    )
    return (
        outs[0].reshape(queries.shape),
        outs[1].reshape(key_vectors.shape),
        outs[2].reshape(value_vectors.shape),
    ) + tuple(outs[3:])


def solution(mesh):
    seq = P("ctx", "tp", None)
    both = P("ctx", "tp")
    ctx = P("ctx", None)
    return jax.shard_map(
        functools.partial(local, mesh.shape["ctx"], mesh.shape["tp"]),
        mesh=mesh,
        in_specs=(seq, seq, seq, seq, seq, both, both, ctx, ctx, both),
        out_specs=(seq, seq, seq, both, ctx, ctx, both),
        check_vma=False,
    )
```

```python
import functools
import math

import jax
import jax.numpy as jnp
from jax import lax
from jax.experimental import pallas as pl
from jax.experimental.pallas import tpu as pltpu
from jax.sharding import PartitionSpec as P

F32 = jnp.float32
BF16 = jnp.bfloat16
MESH = pl.DeviceIdType.MESH
LOG2E = math.log2(math.e)
MASKED = -1e30


def mm(a, b):
    return lax.dot_general(a, b, (((1,), (0,)), ((), ())), preferred_element_type=F32)


def mm_nt(a, b):
    return lax.dot_general(a, b, (((1,), (1,)), ((), ())), preferred_element_type=F32)


def mm_full(a, b):
    return lax.dot_general(
        a, b, (((1,), (0,)), ((), ())), precision=lax.Precision.HIGHEST, preferred_element_type=F32
    )


def halves(a):
    high = a.astype(BF16)
    return high, (a - high.astype(F32)).astype(BF16)


def mm_split(a, b):
    high, low = halves(a)
    return mm(high, b) + mm(low, b)


def mm_nt_split(a, b):
    high, low = halves(a)
    return mm_nt(high, b) + mm_nt(low, b)


def kernel(
    n,
    ntp,
    heads,
    q_hbm,
    k_hbm,
    v_hbm,
    o_hbm,
    go_hbm,
    x_hbm,
    g_hbm,
    bm_hbm,
    cm_hbm,
    dl_hbm,
    gq_hbm,
    gk_hbm,
    gv_hbm,
    gx_hbm,
    gb_hbm,
    gc_hbm,
    gd_hbm,
    gq_ref,
    gk_ref,
    gv_ref,
    gx_ref,
    gb_ref,
    gc_ref,
    gd_ref,
    q_ref,
    o_ref,
    go_ref,
    x_ref,
    g_ref,
    bm_ref,
    cm_ref,
    dl_ref,
    kv,
    st,
    st_out,
    tot,
    grad_out,
    grad_in,
    grad_mid,
    grad_own,
    tp_buf,
    gs,
    xs,
    ends_pre,
    e_wide,
    f_wide,
    half_wide,
    dots_row,
    stat_max,
    stat_sum,
    gq_t,
    load_s,
    store_s,
    kv_s,
    kv_r,
    kv_f,
    st_s,
    st_r,
    st_f,
    tt_s,
    tt_r,
    gr_s,
    gr_r,
    gm_r,
    tp_s,
    tp_r,
):
    me = lax.axis_index("ctx")
    me_tp = lax.axis_index("tp")
    tokens, channels = x_ref.shape
    groups = dl_ref.shape[0]
    state = bm_ref.shape[0]
    column = lax.rem(me, 2)
    level = me // 2
    levels = n // 2
    partner = me + 1 - 2 * column
    rows, width = q_ref.shape
    chunk = 256
    score_scale = 1.0 / math.sqrt(width)

    loads = [
        pltpu.make_async_copy(src, dst, load_s.at[at])
        for at, (src, dst) in enumerate(
            (
                (k_hbm, kv.at[me, pl.ds(0, tokens), :]),
                (v_hbm, kv.at[me, pl.ds(tokens, tokens), :]),
                (dl_hbm, dl_ref),
                (bm_hbm, bm_ref),
                (cm_hbm, cm_ref),
                (g_hbm, g_ref),
                (x_hbm, x_ref),
                (q_hbm, q_ref),
                (go_hbm, go_ref),
                (o_hbm, o_ref),
            )
        )
    ]
    for load in loads:
        load.start()

    stores = [
        pltpu.make_async_copy(src, dst, store_s.at[at])
        for at, (src, dst) in enumerate(
            (
                (gq_ref, gq_hbm),
                (gk_ref, gk_hbm),
                (gv_ref, gv_hbm),
                (gx_ref, gx_hbm),
                (gb_ref, gb_hbm),
                (gc_ref, gc_hbm),
                (gd_ref, gd_hbm),
            )
        )
    ]

    barrier = pltpu.get_barrier_semaphore()

    def greet_ctx(d, c):
        pl.semaphore_signal(
            barrier, inc=1, device_id={"ctx": lax.rem(me + d, n)}, device_id_type=MESH
        )
        return c

    def greet_tp(d, c):
        pl.semaphore_signal(
            barrier, inc=1, device_id={"tp": lax.rem(me_tp + d, ntp)}, device_id_type=MESH
        )
        return c

    lax.fori_loop(1, n, greet_ctx, 0)
    lax.fori_loop(1, ntp, greet_tp, 0)
    loads[0].wait()
    loads[1].wait()
    pl.semaphore_wait(barrier, n - 1 + ntp - 1)

    def kv_copy(src, dst):
        return pltpu.make_async_remote_copy(
            src_ref=kv.at[src],
            dst_ref=kv.at[src],
            send_sem=kv_s.at[dst],
            recv_sem=kv_r.at[src],
            device_id={"ctx": dst},
            device_id_type=MESH,
        )

    def kv_forward(src):
        return pltpu.make_async_remote_copy(
            src_ref=kv.at[src],
            dst_ref=kv.at[src],
            send_sem=kv_f.at[src],
            recv_sem=kv_r.at[src],
            device_id={"ctx": partner},
            device_id_type=MESH,
        )

    def state_forward(src):
        return pltpu.make_async_remote_copy(
            src_ref=st.at[src],
            dst_ref=st.at[src],
            send_sem=st_f.at[src],
            recv_sem=st_r.at[src],
            device_id={"ctx": partner},
            device_id_type=MESH,
        )

    def state_copy(src, dst, which):
        return pltpu.make_async_remote_copy(
            src_ref=st_out.at[which],
            dst_ref=st.at[src],
            send_sem=st_s.at[dst],
            recv_sem=st_r.at[src],
            device_id={"ctx": dst},
            device_id_type=MESH,
        )

    def tot_copy(src, dst):
        return pltpu.make_async_remote_copy(
            src_ref=tot.at[src],
            dst_ref=tot.at[src],
            send_sem=tt_s.at[dst],
            recv_sem=tt_r.at[src],
            device_id={"ctx": dst},
            device_id_type=MESH,
        )

    def grad_copy(src, dst):
        return pltpu.make_async_remote_copy(
            src_ref=grad_out.at[dst],
            dst_ref=grad_in.at[src],
            send_sem=gr_s.at[dst],
            recv_sem=gr_r.at[src],
            device_id={"ctx": dst},
            device_id_type=MESH,
        )

    def grad_pair(dst):
        return pltpu.make_async_remote_copy(
            src_ref=grad_out.at[dst],
            dst_ref=grad_mid.at[dst // 2],
            send_sem=gr_s.at[dst],
            recv_sem=gm_r.at[dst // 2],
            device_id={"ctx": partner},
            device_id_type=MESH,
        )

    def tp_copy(src, dst):
        return pltpu.make_async_remote_copy(
            src_ref=tp_buf.at[src],
            dst_ref=tp_buf.at[src],
            send_sem=tp_s.at[dst],
            recv_sem=tp_r.at[src],
            device_id={"tp": dst},
            device_id_type=MESH,
        )

    @pl.when(column == 0)
    def _():
        kv_copy(me, partner).start()

    def send_kv(d, c):
        kv_copy(me, 2 * (levels - 1 - d) + column).start()
        return c

    lax.fori_loop(0, levels - 1 - level, send_kv, 0)
    for load in loads[2:]:
        load.wait()

    token_row = lax.broadcasted_iota(jnp.int32, (tokens, tokens), 0)
    token_col = lax.broadcasted_iota(jnp.int32, (tokens, tokens), 1)
    lower = token_row >= token_col
    seg = (
        lax.broadcasted_iota(jnp.int32, (groups, channels), 1) // (channels // groups)
        == lax.broadcasted_iota(jnp.int32, (groups, channels), 0)
    ).astype(F32).astype(BF16)

    def tall(wide):
        pad = jnp.zeros((128 - wide.shape[0], tokens), F32)
        return jnp.concatenate([wide, pad], axis=0).T[:, 0 : wide.shape[0]]

    cum = mm_full(lower.astype(F32), tall(dl_ref[...]))
    total = cum[tokens - 1 : tokens, :]
    mid = 0.5 * total
    e_wide[...] = mm_split(jnp.exp(cum - mid), seg)
    f_wide[...] = mm_split(jnp.exp(mid - cum), seg)
    half_wide[...] = mm_split(jnp.exp(jnp.broadcast_to(mid, (state, groups))), seg)
    gs[0:tokens, :] = (e_wide[...] * g_ref[...].astype(F32)).astype(BF16)
    xs[0:tokens, :] = (f_wide[...] * x_ref[...].astype(F32)).astype(BF16)
    in_map_t = bm_ref[...]
    out_map_t = cm_ref[...]
    maps = tall(jnp.concatenate([in_map_t, out_map_t], axis=0))
    in_map = maps[:, 0:state]
    out_map = maps[:, state : 2 * state]
    ends_pre[...] = mm_split(in_map_t, xs[0:tokens, :])
    st_out[0] = (half_wide[...] * ends_pre[...]).astype(BF16)
    st_out[1] = (half_wide[...] * mm_split(out_map_t, gs[0:tokens, :])).astype(BF16)
    tot[me] = jnp.broadcast_to(
        jnp.concatenate([total, jnp.zeros((1, 128 - groups), F32)], axis=1), (8, 128)
    )

    def send_tot(d, c):
        tot_copy(me, lax.rem(me + d, n)).start()
        return c

    def send_ends(d, c):
        state_copy(me, 2 * (levels - 1 - d) + column, 0).start()
        return c

    def send_pulls(at, c):
        state_copy(me, 2 * at + column, 1).start()
        return c

    lax.fori_loop(1, n, send_tot, 0)
    state_copy(me, partner, column).start()
    lax.fori_loop(0, levels - 1 - level, send_ends, 0)
    lax.fori_loop(0, level, send_pulls, 0)

    key_at = lax.broadcasted_iota(jnp.int32, (tokens, chunk), 0)
    pair_at = lax.broadcasted_iota(jnp.int32, (tokens, chunk), 1)
    ones_row = jnp.ones((8, width), BF16)

    for first in range(0, rows, chunk):
        part = pl.ds(first, chunk)
        prod = go_ref[part, :].astype(F32) * o_ref[part, :].astype(F32)
        high, low = halves(prod)
        dots_row[:, part] = mm_nt(ones_row, high) + mm_nt(ones_row, low)

    def scores_of(keys, first, diagonal):
        scores = mm_nt(keys, q_ref[pl.ds(first, chunk), :]) * (score_scale * LOG2E)
        if diagonal:
            scores = jnp.where(key_at <= (pair_at + first) // heads, scores, MASKED)
        return scores

    own_keys = kv[me, 0:tokens, :]
    for first in range(0, rows, chunk):
        part = pl.ds(first, chunk)
        scores = scores_of(own_keys, first, True)
        top = jnp.max(scores, axis=0, keepdims=True)
        stat_max[:, part] = jnp.broadcast_to(top, (8, chunk))
        stat_sum[:, part] = jnp.broadcast_to(
            jnp.sum(jnp.exp2(scores - top), axis=0, keepdims=True), (8, chunk)
        )

    def stats_of(src):
        keys = kv[src, 0:tokens, :]
        for first in range(0, rows, chunk):
            part = pl.ds(first, chunk)
            scores = scores_of(keys, first, False)
            before = stat_max[0:1, part]
            top = jnp.maximum(before, jnp.max(scores, axis=0, keepdims=True))
            summed = stat_sum[0:1, part] * jnp.exp2(before - top) + jnp.sum(
                jnp.exp2(scores - top), axis=0, keepdims=True
            )
            stat_max[:, part] = jnp.broadcast_to(top, (8, chunk))
            stat_sum[:, part] = jnp.broadcast_to(summed, (8, chunk))

    def stats_step(d, c):
        src = 2 * (level - d) + column
        across = 2 * (level - d + 1) + 1 - column
        kv_copy(src, me).wait_recv()
        kv_forward(src).start()
        stats_of(src)

        @pl.when(across < me)
        def _():
            kv_copy(across, me).wait_recv()
            stats_of(across)

        return c

    lax.fori_loop(1, level + 1, stats_step, 0)

    @pl.when(me > 0)
    def _():
        kv_copy(1 - column, me).wait_recv()
        stats_of(1 - column)

    stat_max[...] = stat_max[...] + jnp.log(stat_sum[...]) * LOG2E
    gq_t[...] = jnp.zeros_like(gq_t)

    def grads_of(keys, values, diagonal):
        keys_t = keys.astype(F32).T.astype(BF16)
        key_sum = jnp.zeros((tokens, width), F32)
        value_sum = jnp.zeros((tokens, width), F32)
        for first in range(0, rows, chunk):
            part = pl.ds(first, chunk)
            queries = q_ref[part, :]
            grads = go_ref[part, :]
            probs = jnp.exp2(scores_of(keys, first, diagonal) - stat_max[0:1, part])
            grad_probs = mm_nt(values, grads)
            grad_scores = (probs * (grad_probs - dots_row[0:1, part]) * score_scale).astype(BF16)
            value_sum = value_sum + mm(probs.astype(BF16), grads)
            key_sum = key_sum + mm(grad_scores, queries)
            gq_t[:, part] += mm(keys_t, grad_scores)
        return key_sum, value_sum

    def grads_across(src):
        key_sum, value_sum = grads_of(kv[src, 0:tokens, :], kv[src, tokens : 2 * tokens, :], False)
        grad_out[src, 0:tokens, :] = key_sum.astype(BF16)
        grad_out[src, tokens : 2 * tokens, :] = value_sum.astype(BF16)

    def pass_on(at):
        dst = 2 * at + column
        grad_pair(dst).wait_recv()
        grad_out[dst] = (grad_own[at] + grad_mid[at].astype(F32)).astype(BF16)
        grad_copy(me, dst).start()

    def grads_step(at, c):
        across = 2 * at + 1 - column
        grads_across(across)
        grad_pair(across).start()
        src = 2 * at + column
        key_sum, value_sum = grads_of(kv[src, 0:tokens, :], kv[src, tokens : 2 * tokens, :], False)
        grad_own[at, 0:tokens, :] = key_sum
        grad_own[at, tokens : 2 * tokens, :] = value_sum

        @pl.when(at > 0)
        def _():
            pass_on(at - 1)

        return c

    lax.fori_loop(0, level, grads_step, 0)

    @pl.when(column == 1)
    def _():
        grads_across(partner)
        grad_copy(me, partner).start()

    @pl.when(level > 0)
    def _():
        pass_on(level - 1)

    def forward_states(d, c):
        src = lax.rem(me + 2 * d, n)
        state_copy(src, me, 0).wait_recv()
        state_forward(src).start()
        return c

    lax.fori_loop(1, levels, forward_states, 0)
    own_key_sum, own_value_sum = grads_of(own_keys, kv[me, tokens : 2 * tokens, :], True)
    gq_ref[...] = gq_t[...].T.astype(BF16)
    stores[0].start()

    def take_states(start, src_of):
        def step(d, carry):
            summed, log_sum = carry
            src = src_of(d)
            tot_copy(src, me).wait_recv()

            @pl.when(lax.rem(src, 2) != column)
            def _():
                state_copy(src, me, 0).wait_recv()

            summed = summed + mm_split(jnp.exp(log_sum), seg) * st[src].astype(F32)
            log_sum = log_sum + jnp.broadcast_to(tot[src][0:1, 0:groups], (state, groups))
            return summed, log_sum

        zero = (jnp.zeros((state, channels), F32), jnp.zeros((state, groups), F32))
        return lax.fori_loop(1, start, step, zero)[0]

    state_in = take_states(me + 1, lambda d: me - d) * half_wide[...]
    pull_in = take_states(n - me, lambda d: me + d) * half_wide[...]
    for ref, arrived in ((xs, state_in), (gs, pull_in)):
        high, low = halves(arrived)
        ref[tokens : tokens + state, :] = high
        ref[tokens + state : tokens + 2 * state, :] = low
    kernel_sum = jnp.where(lower, mm_nt(gs[0:tokens, :], xs[0:tokens, :]), 0.0)
    pulled = mm_nt(gs[tokens : tokens + 2 * state, :], xs[0:tokens, :])
    carried = mm_nt(xs[tokens : tokens + 2 * state, :], gs[0:tokens, :])
    tp_buf[me_tp, 0:state, :] = (
        mm_full(out_map_t, kernel_sum) + pulled[0:state] + pulled[state : 2 * state]
    )
    tp_buf[me_tp, state : 2 * state, :] = (
        mm_full(in_map_t, kernel_sum.T) + carried[0:state] + carried[state : 2 * state]
    )

    def send_tp(d, c):
        tp_copy(me_tp, lax.rem(me_tp + d, ntp)).start()
        return c

    lax.fori_loop(1, ntp, send_tp, 0)

    map_dots = jnp.where(lower, mm_full(out_map, in_map_t), 0.0)
    forward = jnp.concatenate([map_dots, out_map, out_map], axis=1)
    backward = jnp.concatenate([map_dots.T, in_map, in_map], axis=1)
    out_pre = mm_split(forward, xs[...])
    in_pre = mm_split(backward, gs[...])
    gx_ref[...] = (f_wide[...] * in_pre).astype(BF16)
    stores[3].start()
    per_token = gs[0:tokens, :].astype(F32) * out_pre - xs[0:tokens, :].astype(F32) * in_pre
    at_end = pull_in * (state_in + ends_pre[...])
    seg_token = mm_nt_split(per_token, seg)
    seg_end = mm_nt_split(at_end, seg)
    grad_decay = mm_full((token_row <= token_col).astype(F32), seg_token) + jnp.sum(
        seg_end, axis=0, keepdims=True
    )
    gd_ref[...] = jnp.concatenate(
        [grad_decay, jnp.zeros((tokens, 128 - groups), F32)], axis=1
    ).T[0:groups, :]
    stores[6].start()

    @pl.when(column == 0)
    def _():
        grad_copy(partner, me).wait_recv()

    @pl.when(column == 1)
    def _():
        grad_in[partner] = jnp.zeros((2 * tokens, width), BF16)

    def take_grads(at, carry):
        src = 2 * at + column
        grad_copy(src, me).wait_recv()
        return (
            carry[0] + grad_in[src, 0:tokens, :].astype(F32),
            carry[1] + grad_in[src, tokens : 2 * tokens, :].astype(F32),
        )

    key_total, value_total = lax.fori_loop(
        level + 1,
        levels,
        take_grads,
        (
            own_key_sum + grad_in[partner, 0:tokens, :].astype(F32),
            own_value_sum + grad_in[partner, tokens : 2 * tokens, :].astype(F32),
        ),
    )
    gk_ref[...] = key_total.astype(BF16)
    gv_ref[...] = value_total.astype(BF16)
    stores[1].start()
    stores[2].start()

    def wait_tp(d, c):
        tp_copy(lax.rem(me_tp + d, ntp), me_tp).wait_recv()
        return c

    lax.fori_loop(1, ntp, wait_tp, 0)
    map_grads = tp_buf[0]
    for other in range(1, ntp):
        map_grads = map_grads + tp_buf[other]
    gb_ref[...] = map_grads[0:state, :]
    gc_ref[...] = map_grads[state : 2 * state, :]
    stores[4].start()
    stores[5].start()

    def end_tp(d, c):
        tp_copy(me_tp, lax.rem(me_tp + d, ntp)).wait_send()
        return c

    def end_tot(d, c):
        tot_copy(me, lax.rem(me + d, n)).wait_send()
        return c

    def end_states(d, c):
        other = lax.rem(me + 2 * d, n)
        state_copy(me, other, 0).wait_send()
        state_forward(other).wait_send()
        return c

    def end_kv(at, c):
        kv_copy(me, 2 * at + column).wait_send()
        return c

    def end_kv_forward(at, c):
        kv_forward(2 * at + column).wait_send()
        return c

    def end_grads(dst, c):
        grad_copy(me, dst).wait_send()
        return c

    lax.fori_loop(1, ntp, end_tp, 0)
    lax.fori_loop(1, n, end_tot, 0)
    state_copy(me, partner, 0).wait_send()
    lax.fori_loop(1, levels, end_states, 0)

    @pl.when(column == 0)
    def _():
        kv_copy(me, partner).wait_send()

    lax.fori_loop(level + 1, levels, end_kv, 0)
    lax.fori_loop(0, level, end_kv_forward, 0)
    lax.fori_loop(0, me, end_grads, 0)
    for store in stores:
        store.wait()


def write_out(*refs):
    count = len(refs) // 2
    sems = refs[-1]
    copies = [
        pltpu.make_async_copy(refs[at], refs[count + at], sems.at[at]) for at in range(count)
    ]
    for copy in copies:
        copy.start()
    for copy in copies:
        copy.wait()


def local(
    n,
    ntp,
    queries,
    key_vectors,
    value_vectors,
    attention_out,
    grad_attention,
    mix_input,
    grad_mix,
    input_map,
    output_map,
    decay_log,
):
    tokens, heads, width = queries.shape
    channels = mix_input.shape[1]
    state = input_map.shape[1]
    groups = decay_log.shape[1]
    rows = tokens * heads
    flat = lambda a: a.reshape(-1, width)
    hbm = pl.BlockSpec(memory_space=pltpu.HBM)
    dma = pltpu.SemaphoreType.DMA
    shapes = (
        jax.ShapeDtypeStruct((rows, width), BF16),
        jax.ShapeDtypeStruct((tokens, width), BF16),
        jax.ShapeDtypeStruct((tokens, width), BF16),
        jax.ShapeDtypeStruct((tokens, channels), BF16),
        jax.ShapeDtypeStruct((state, tokens), F32),
        jax.ShapeDtypeStruct((state, tokens), F32),
        jax.ShapeDtypeStruct((groups, tokens), F32),
    )
    outs = pl.pallas_call(
        functools.partial(kernel, n, ntp, heads),
        out_shape=shapes,
        in_specs=[hbm] * 10,
        out_specs=(hbm,) * 7,
        scratch_shapes=[pltpu.VMEM(out.shape, out.dtype) for out in shapes]
        + [
            pltpu.VMEM((rows, width), BF16),
            pltpu.VMEM((rows, width), BF16),
            pltpu.VMEM((rows, width), BF16),
            pltpu.VMEM((tokens, channels), BF16),
            pltpu.VMEM((tokens, channels), BF16),
            pltpu.VMEM((state, tokens), F32),
            pltpu.VMEM((state, tokens), F32),
            pltpu.VMEM((groups, tokens), F32),
            pltpu.VMEM((n, 2 * tokens, width), BF16),
            pltpu.VMEM((n, state, channels), BF16),
            pltpu.VMEM((2, state, channels), BF16),
            pltpu.VMEM((n, 8, 128), F32),
            pltpu.VMEM((n, 2 * tokens, width), BF16),
            pltpu.VMEM((n, 2 * tokens, width), BF16),
            pltpu.VMEM((n // 2, 2 * tokens, width), BF16),
            pltpu.VMEM((n // 2, 2 * tokens, width), F32),
            pltpu.VMEM((ntp, 2 * state, tokens), F32),
            pltpu.VMEM((tokens + 2 * state, channels), BF16),
            pltpu.VMEM((tokens + 2 * state, channels), BF16),
            pltpu.VMEM((state, channels), F32),
            pltpu.VMEM((tokens, channels), F32),
            pltpu.VMEM((tokens, channels), F32),
            pltpu.VMEM((state, channels), F32),
            pltpu.VMEM((8, rows), F32),
            pltpu.VMEM((8, rows), F32),
            pltpu.VMEM((8, rows), F32),
            pltpu.VMEM((width, rows), F32),
            dma((10,)),
            dma((7,)),
            dma((n,)),
            dma((n,)),
            dma((n,)),
            dma((n,)),
            dma((n,)),
            dma((n,)),
            dma((n,)),
            dma((n,)),
            dma((n,)),
            dma((n,)),
            dma((n // 2,)),
            dma((ntp,)),
            dma((ntp,)),
        ],
        compiler_params=pltpu.CompilerParams(
            collective_id=0, has_side_effects=True, vmem_limit_bytes=63 * 1024 * 1024
        ),
        name="layer_grads",
    )(
        flat(queries),
        flat(key_vectors),
        flat(value_vectors),
        flat(attention_out),
        flat(grad_attention),
        mix_input,
        grad_mix,
        input_map.T,
        output_map.T,
        decay_log.T,
    )
    outs = pl.pallas_call(
        write_out,
        out_shape=shapes,
        in_specs=[hbm] * 7,
        out_specs=(hbm,) * 7,
        compiler_params=pltpu.CompilerParams(vmem_limit_bytes=63 * 1024 * 1024),
        scratch_shapes=[dma((7,))],
        name="write_out",
    )(*outs)
    return (
        outs[0].reshape(queries.shape),
        outs[1].reshape(key_vectors.shape),
        outs[2].reshape(value_vectors.shape),
        outs[3], outs[4].T, outs[5].T, outs[6].T)


def solution(mesh):
    seq = P("ctx", "tp", None)
    both = P("ctx", "tp")
    ctx = P("ctx", None)
    return jax.shard_map(
        functools.partial(local, mesh.shape["ctx"], mesh.shape["tp"]),
        mesh=mesh,
        in_specs=(seq, seq, seq, seq, seq, both, both, ctx, ctx, both),
        out_specs=(seq, seq, seq, both, ctx, ctx, both),
        check_vma=False,
    )
```

```python
import functools
import math

import jax
import jax.numpy as jnp
from jax import lax
from jax.experimental import pallas as pl
from jax.experimental.pallas import tpu as pltpu
from jax.sharding import PartitionSpec as P

F32 = jnp.float32
BF16 = jnp.bfloat16
MESH = pl.DeviceIdType.MESH
LOG2E = math.log2(math.e)
MASKED = -1e30


def mm(a, b):
    return lax.dot_general(a, b, (((1,), (0,)), ((), ())), preferred_element_type=F32)


def mm_nt(a, b):
    return lax.dot_general(a, b, (((1,), (1,)), ((), ())), preferred_element_type=F32)


def mm_full(a, b):
    return lax.dot_general(
        a, b, (((1,), (0,)), ((), ())), precision=lax.Precision.HIGHEST, preferred_element_type=F32
    )


def halves(a):
    high = a.astype(BF16)
    return high, (a - high.astype(F32)).astype(BF16)


def mm_split(a, b):
    high, low = halves(a)
    return mm(high, b) + mm(low, b)


def mm_nt_split(a, b):
    high, low = halves(a)
    return mm_nt(high, b) + mm_nt(low, b)


def kernel(
    n,
    ntp,
    heads,
    q_hbm,
    k_hbm,
    v_hbm,
    o_hbm,
    go_hbm,
    x_hbm,
    g_hbm,
    bm_hbm,
    cm_hbm,
    dl_hbm,
    gq_hbm,
    gk_hbm,
    gv_hbm,
    gx_hbm,
    gb_hbm,
    gc_hbm,
    gd_hbm,
    gq_ref,
    gk_ref,
    gv_ref,
    gx_ref,
    gb_ref,
    gc_ref,
    gd_ref,
    q_ref,
    o_ref,
    go_ref,
    x_ref,
    g_ref,
    bm_ref,
    cm_ref,
    dl_ref,
    kv,
    st,
    st_out,
    tot,
    grad_out,
    grad_in,
    grad_mid,
    grad_own,
    tp_buf,
    gs,
    xs,
    ends_pre,
    e_wide,
    f_wide,
    half_wide,
    carry_wide,
    out_own,
    in_own,
    maps_own,
    dots_row,
    stat_max,
    stat_sum,
    gq_t,
    load_s,
    store_s,
    kv_s,
    kv_r,
    kv_f,
    st_s,
    st_r,
    st_f,
    tt_s,
    tt_r,
    gr_s,
    gr_r,
    gm_r,
    tp_s,
    tp_r,
):
    me = lax.axis_index("ctx")
    me_tp = lax.axis_index("tp")
    tokens, channels = x_ref.shape
    groups = dl_ref.shape[0]
    state = bm_ref.shape[0]
    column = lax.rem(me, 2)
    level = me // 2
    levels = n // 2
    partner = me + 1 - 2 * column
    rows, width = q_ref.shape
    chunk = 256
    score_scale = 1.0 / math.sqrt(width)

    loads = [
        pltpu.make_async_copy(src, dst, load_s.at[at])
        for at, (src, dst) in enumerate(
            (
                (k_hbm, kv.at[me, pl.ds(0, tokens), :]),
                (v_hbm, kv.at[me, pl.ds(tokens, tokens), :]),
                (dl_hbm, dl_ref),
                (bm_hbm, bm_ref),
                (cm_hbm, cm_ref),
                (g_hbm, g_ref),
                (x_hbm, x_ref),
                (q_hbm, q_ref),
                (go_hbm, go_ref),
                (o_hbm, o_ref),
            )
        )
    ]
    for load in loads:
        load.start()

    stores = [
        pltpu.make_async_copy(src, dst, store_s.at[at])
        for at, (src, dst) in enumerate(
            (
                (gq_ref, gq_hbm),
                (gk_ref, gk_hbm),
                (gv_ref, gv_hbm),
                (gx_ref, gx_hbm),
                (gb_ref, gb_hbm),
                (gc_ref, gc_hbm),
                (gd_ref, gd_hbm),
            )
        )
    ]

    barrier = pltpu.get_barrier_semaphore()

    def greet_ctx(d, c):
        pl.semaphore_signal(
            barrier, inc=1, device_id={"ctx": lax.rem(me + d, n)}, device_id_type=MESH
        )
        return c

    def greet_tp(d, c):
        pl.semaphore_signal(
            barrier, inc=1, device_id={"tp": lax.rem(me_tp + d, ntp)}, device_id_type=MESH
        )
        return c

    lax.fori_loop(1, n, greet_ctx, 0)
    lax.fori_loop(1, ntp, greet_tp, 0)
    loads[0].wait()
    loads[1].wait()
    pl.semaphore_wait(barrier, n - 1 + ntp - 1)

    def kv_copy(src, dst):
        return pltpu.make_async_remote_copy(
            src_ref=kv.at[src],
            dst_ref=kv.at[src],
            send_sem=kv_s.at[dst],
            recv_sem=kv_r.at[src],
            device_id={"ctx": dst},
            device_id_type=MESH,
        )

    def kv_forward(src):
        return pltpu.make_async_remote_copy(
            src_ref=kv.at[src],
            dst_ref=kv.at[src],
            send_sem=kv_f.at[src],
            recv_sem=kv_r.at[src],
            device_id={"ctx": partner},
            device_id_type=MESH,
        )

    def state_forward(src):
        return pltpu.make_async_remote_copy(
            src_ref=st.at[src],
            dst_ref=st.at[src],
            send_sem=st_f.at[src],
            recv_sem=st_r.at[src],
            device_id={"ctx": partner},
            device_id_type=MESH,
        )

    def state_copy(src, dst, which):
        return pltpu.make_async_remote_copy(
            src_ref=st_out.at[which],
            dst_ref=st.at[src],
            send_sem=st_s.at[dst],
            recv_sem=st_r.at[src],
            device_id={"ctx": dst},
            device_id_type=MESH,
        )

    def tot_copy(src, dst):
        return pltpu.make_async_remote_copy(
            src_ref=tot.at[src],
            dst_ref=tot.at[src],
            send_sem=tt_s.at[dst],
            recv_sem=tt_r.at[src],
            device_id={"ctx": dst},
            device_id_type=MESH,
        )

    def grad_copy(src, dst):
        return pltpu.make_async_remote_copy(
            src_ref=grad_out.at[dst],
            dst_ref=grad_in.at[src],
            send_sem=gr_s.at[dst],
            recv_sem=gr_r.at[src],
            device_id={"ctx": dst},
            device_id_type=MESH,
        )

    def grad_pair(dst):
        return pltpu.make_async_remote_copy(
            src_ref=grad_out.at[dst],
            dst_ref=grad_mid.at[dst // 2],
            send_sem=gr_s.at[dst],
            recv_sem=gm_r.at[dst // 2],
            device_id={"ctx": partner},
            device_id_type=MESH,
        )

    def tp_copy(src, dst):
        return pltpu.make_async_remote_copy(
            src_ref=tp_buf.at[src],
            dst_ref=tp_buf.at[src],
            send_sem=tp_s.at[dst],
            recv_sem=tp_r.at[src],
            device_id={"tp": dst},
            device_id_type=MESH,
        )

    @pl.when(column == 0)
    def _():
        kv_copy(me, partner).start()

    def send_kv(d, c):
        kv_copy(me, 2 * (levels - 1 - d) + column).start()
        return c

    lax.fori_loop(0, levels - 1 - level, send_kv, 0)
    for load in loads[2:]:
        load.wait()

    token_row = lax.broadcasted_iota(jnp.int32, (tokens, tokens), 0)
    token_col = lax.broadcasted_iota(jnp.int32, (tokens, tokens), 1)
    lower = token_row >= token_col
    seg = (
        lax.broadcasted_iota(jnp.int32, (groups, channels), 1) // (channels // groups)
        == lax.broadcasted_iota(jnp.int32, (groups, channels), 0)
    ).astype(F32).astype(BF16)

    def tall(wide):
        pad = jnp.zeros((128 - wide.shape[0], tokens), F32)
        return jnp.concatenate([wide, pad], axis=0).T[:, 0 : wide.shape[0]]

    cum = mm_full(lower.astype(F32), tall(dl_ref[...]))
    total = cum[tokens - 1 : tokens, :]
    mid = 0.5 * total
    e_wide[...] = mm_split(jnp.exp(cum - mid), seg)
    f_wide[...] = mm_split(jnp.exp(mid - cum), seg)
    half_wide[...] = mm_split(jnp.exp(jnp.broadcast_to(mid, (state, groups))), seg)
    gs[0:tokens, :] = (e_wide[...] * g_ref[...].astype(F32)).astype(BF16)
    xs[0:tokens, :] = (f_wide[...] * x_ref[...].astype(F32)).astype(BF16)
    in_map_t = bm_ref[...]
    out_map_t = cm_ref[...]
    maps = tall(jnp.concatenate([in_map_t, out_map_t], axis=0))
    in_map = maps[:, 0:state]
    out_map = maps[:, state : 2 * state]
    ends_pre[...] = mm_split(in_map_t, xs[0:tokens, :])
    st_out[0] = (half_wide[...] * ends_pre[...]).astype(BF16)
    st_out[1] = (half_wide[...] * mm_split(out_map_t, gs[0:tokens, :])).astype(BF16)
    tot[me] = jnp.broadcast_to(
        jnp.concatenate([total, jnp.zeros((1, 128 - groups), F32)], axis=1), (8, 128)
    )

    def send_tot(d, c):
        tot_copy(me, lax.rem(me + d, n)).start()
        return c

    def send_ends(d, c):
        state_copy(me, 2 * (levels - 1 - d) + column, 0).start()
        return c

    def send_pulls(at, c):
        state_copy(me, 2 * at + column, 1).start()
        return c

    lax.fori_loop(1, n, send_tot, 0)
    state_copy(me, partner, column).start()
    lax.fori_loop(0, levels - 1 - level, send_ends, 0)
    lax.fori_loop(0, level, send_pulls, 0)

    key_at = lax.broadcasted_iota(jnp.int32, (tokens, chunk), 0)
    pair_at = lax.broadcasted_iota(jnp.int32, (tokens, chunk), 1)
    ones_row = jnp.ones((8, width), BF16)

    for first in range(0, rows, chunk):
        part = pl.ds(first, chunk)
        prod = go_ref[part, :].astype(F32) * o_ref[part, :].astype(F32)
        high, low = halves(prod)
        dots_row[:, part] = mm_nt(ones_row, high) + mm_nt(ones_row, low)

    def scores_of(keys, first, diagonal):
        scores = mm_nt(keys, q_ref[pl.ds(first, chunk), :]) * (score_scale * LOG2E)
        if diagonal:
            scores = jnp.where(key_at <= (pair_at + first) // heads, scores, MASKED)
        return scores

    own_keys = kv[me, 0:tokens, :]
    for first in range(0, rows, chunk):
        part = pl.ds(first, chunk)
        scores = scores_of(own_keys, first, True)
        top = jnp.max(scores, axis=0, keepdims=True)
        stat_max[:, part] = jnp.broadcast_to(top, (8, chunk))
        stat_sum[:, part] = jnp.broadcast_to(
            jnp.sum(jnp.exp2(scores - top), axis=0, keepdims=True), (8, chunk)
        )

    kernel_sum = jnp.where(lower, mm_nt(gs[0:tokens, :], xs[0:tokens, :]), 0.0)
    maps_own[0:state, :] = mm_full(out_map_t, kernel_sum)
    maps_own[state : 2 * state, :] = mm_full(in_map_t, kernel_sum.T)
    map_dots = jnp.where(lower, mm_full(out_map, in_map_t), 0.0)
    out_own[...] = mm_split(map_dots, xs[0:tokens, :])
    in_own[...] = mm_split(map_dots.T, gs[0:tokens, :])

    def stats_of(src):
        keys = kv[src, 0:tokens, :]
        for first in range(0, rows, chunk):
            part = pl.ds(first, chunk)
            scores = scores_of(keys, first, False)
            before = stat_max[0:1, part]
            top = jnp.maximum(before, jnp.max(scores, axis=0, keepdims=True))
            summed = stat_sum[0:1, part] * jnp.exp2(before - top) + jnp.sum(
                jnp.exp2(scores - top), axis=0, keepdims=True
            )
            stat_max[:, part] = jnp.broadcast_to(top, (8, chunk))
            stat_sum[:, part] = jnp.broadcast_to(summed, (8, chunk))

    def stats_step(d, c):
        src = 2 * (level - d) + column
        across = 2 * (level - d + 1) + 1 - column
        kv_copy(src, me).wait_recv()
        kv_forward(src).start()
        stats_of(src)

        @pl.when(across < me)
        def _():
            kv_copy(across, me).wait_recv()
            stats_of(across)

        return c

    lax.fori_loop(1, level + 1, stats_step, 0)

    @pl.when(me > 0)
    def _():
        kv_copy(1 - column, me).wait_recv()
        stats_of(1 - column)

    stat_max[...] = stat_max[...] + jnp.log(stat_sum[...]) * LOG2E
    gq_t[...] = jnp.zeros_like(gq_t)

    def grads_of(keys, values, diagonal):
        keys_t = keys.astype(F32).T.astype(BF16)
        key_sum = jnp.zeros((tokens, width), F32)
        value_sum = jnp.zeros((tokens, width), F32)
        for first in range(0, rows, chunk):
            part = pl.ds(first, chunk)
            queries = q_ref[part, :]
            grads = go_ref[part, :]
            probs = jnp.exp2(scores_of(keys, first, diagonal) - stat_max[0:1, part])
            grad_probs = mm_nt(values, grads)
            grad_scores = (probs * (grad_probs - dots_row[0:1, part]) * score_scale).astype(BF16)
            value_sum = value_sum + mm(probs.astype(BF16), grads)
            key_sum = key_sum + mm(grad_scores, queries)
            gq_t[:, part] += mm(keys_t, grad_scores)
        return key_sum, value_sum

    def grads_across(src):
        key_sum, value_sum = grads_of(kv[src, 0:tokens, :], kv[src, tokens : 2 * tokens, :], False)
        grad_out[src, 0:tokens, :] = key_sum.astype(BF16)
        grad_out[src, tokens : 2 * tokens, :] = value_sum.astype(BF16)

    def pass_on(at):
        dst = 2 * at + column
        grad_pair(dst).wait_recv()
        grad_out[dst] = (grad_own[at] + grad_mid[at].astype(F32)).astype(BF16)
        grad_copy(me, dst).start()

    def forward_states(d, c):
        src = lax.rem(me + 2 * d, n)
        state_copy(src, me, 0).wait_recv()
        state_forward(src).start()
        return c

    def grads_step(at, c):
        across = 2 * at + 1 - column
        grads_across(across)
        grad_pair(across).start()
        src = 2 * at + column
        key_sum, value_sum = grads_of(kv[src, 0:tokens, :], kv[src, tokens : 2 * tokens, :], False)
        grad_own[at, 0:tokens, :] = key_sum
        grad_own[at, tokens : 2 * tokens, :] = value_sum

        @pl.when(at > 0)
        def _():
            pass_on(at - 1)

        return forward_states(at + 1, c)

    lax.fori_loop(0, level, grads_step, 0)
    lax.fori_loop(level + 1, levels, forward_states, 0)

    @pl.when(column == 1)
    def _():
        grads_across(partner)
        grad_copy(me, partner).start()

    @pl.when(level > 0)
    def _():
        pass_on(level - 1)

    own_key_sum, own_value_sum = grads_of(own_keys, kv[me, tokens : 2 * tokens, :], True)
    gq_ref[...] = gq_t[...].T.astype(BF16)
    stores[0].start()

    def wait_tot(d, c):
        tot_copy(lax.rem(me + d, n), me).wait_recv()
        return c

    lax.fori_loop(1, n, wait_tot, 0)
    source = lax.broadcasted_iota(jnp.int32, (n, n), 0)
    passed = lax.broadcasted_iota(jnp.int32, (n, n), 1)
    between = ((source < passed) & (passed < me)) | ((me < passed) & (passed < source))
    carry_log = mm_full(between.astype(F32), tot[:, 0, :])[:, 0:groups]
    carry_wide[...] = mm_split(jnp.exp(carry_log), seg)

    def take_states(src, summed):
        @pl.when(lax.rem(src, 2) != column)
        def _():
            state_copy(src, me, 0).wait_recv()

        return summed + carry_wide[pl.ds(src, 1), :] * st[src].astype(F32)

    nothing = jnp.zeros((state, channels), F32)
    state_in = lax.fori_loop(0, me, take_states, nothing) * half_wide[...]
    pull_in = lax.fori_loop(me + 1, n, take_states, nothing) * half_wide[...]
    for ref, arrived in ((xs, state_in), (gs, pull_in)):
        high, low = halves(arrived)
        ref[tokens : tokens + state, :] = high
        ref[tokens + state : tokens + 2 * state, :] = low
    pulled = mm_nt(gs[tokens : tokens + 2 * state, :], xs[0:tokens, :])
    carried = mm_nt(xs[tokens : tokens + 2 * state, :], gs[0:tokens, :])
    tp_buf[me_tp, 0:state, :] = (
        maps_own[0:state, :] + pulled[0:state] + pulled[state : 2 * state]
    )
    tp_buf[me_tp, state : 2 * state, :] = (
        maps_own[state : 2 * state, :] + carried[0:state] + carried[state : 2 * state]
    )

    def send_tp(d, c):
        tp_copy(me_tp, lax.rem(me_tp + d, ntp)).start()
        return c

    lax.fori_loop(1, ntp, send_tp, 0)

    from_state = jnp.concatenate([out_map, out_map], axis=1)
    from_pull = jnp.concatenate([in_map, in_map], axis=1)
    out_pre = out_own[...] + mm_split(from_state, xs[tokens : tokens + 2 * state, :])
    in_pre = in_own[...] + mm_split(from_pull, gs[tokens : tokens + 2 * state, :])
    gx_ref[...] = (f_wide[...] * in_pre).astype(BF16)
    stores[3].start()
    per_token = gs[0:tokens, :].astype(F32) * out_pre - xs[0:tokens, :].astype(F32) * in_pre
    at_end = pull_in * (state_in + ends_pre[...])
    seg_token = mm_nt_split(per_token, seg)
    seg_end = mm_nt_split(at_end, seg)
    grad_decay = mm_full((token_row <= token_col).astype(F32), seg_token) + jnp.sum(
        seg_end, axis=0, keepdims=True
    )
    gd_ref[...] = jnp.concatenate(
        [grad_decay, jnp.zeros((tokens, 128 - groups), F32)], axis=1
    ).T[0:groups, :]
    stores[6].start()

    @pl.when(column == 0)
    def _():
        grad_copy(partner, me).wait_recv()

    @pl.when(column == 1)
    def _():
        grad_in[partner] = jnp.zeros((2 * tokens, width), BF16)

    def take_grads(at, carry):
        src = 2 * at + column
        grad_copy(src, me).wait_recv()
        return (
            carry[0] + grad_in[src, 0:tokens, :].astype(F32),
            carry[1] + grad_in[src, tokens : 2 * tokens, :].astype(F32),
        )

    key_total, value_total = lax.fori_loop(
        level + 1,
        levels,
        take_grads,
        (
            own_key_sum + grad_in[partner, 0:tokens, :].astype(F32),
            own_value_sum + grad_in[partner, tokens : 2 * tokens, :].astype(F32),
        ),
    )
    gk_ref[...] = key_total.astype(BF16)
    gv_ref[...] = value_total.astype(BF16)
    stores[1].start()
    stores[2].start()

    def wait_tp(d, c):
        tp_copy(lax.rem(me_tp + d, ntp), me_tp).wait_recv()
        return c

    lax.fori_loop(1, ntp, wait_tp, 0)
    map_grads = tp_buf[0]
    for other in range(1, ntp):
        map_grads = map_grads + tp_buf[other]
    gb_ref[...] = map_grads[0:state, :]
    gc_ref[...] = map_grads[state : 2 * state, :]
    stores[4].start()
    stores[5].start()

    def end_tp(d, c):
        tp_copy(me_tp, lax.rem(me_tp + d, ntp)).wait_send()
        return c

    def end_tot(d, c):
        tot_copy(me, lax.rem(me + d, n)).wait_send()
        return c

    def end_states(d, c):
        other = lax.rem(me + 2 * d, n)
        state_copy(me, other, 0).wait_send()
        state_forward(other).wait_send()
        return c

    def end_kv(at, c):
        kv_copy(me, 2 * at + column).wait_send()
        return c

    def end_kv_forward(at, c):
        kv_forward(2 * at + column).wait_send()
        return c

    def end_grads(dst, c):
        grad_copy(me, dst).wait_send()
        return c

    lax.fori_loop(1, ntp, end_tp, 0)
    lax.fori_loop(1, n, end_tot, 0)
    state_copy(me, partner, 0).wait_send()
    lax.fori_loop(1, levels, end_states, 0)

    @pl.when(column == 0)
    def _():
        kv_copy(me, partner).wait_send()

    lax.fori_loop(level + 1, levels, end_kv, 0)
    lax.fori_loop(0, level, end_kv_forward, 0)
    lax.fori_loop(0, me, end_grads, 0)
    for store in stores:
        store.wait()


def write_out(*refs):
    count = len(refs) // 3
    ins, outs, held = refs[:count], refs[count : 2 * count], refs[2 * count : 3 * count]
    sems = refs[-1]
    arrive = [pltpu.make_async_copy(ins[at], held[at], sems.at[0, at]) for at in range(count)]
    leave = [pltpu.make_async_copy(held[at], outs[at], sems.at[1, at]) for at in range(count)]
    for copy in arrive:
        copy.start()
    for at in range(count):
        arrive[at].wait()
        leave[at].start()
    for copy in leave:
        copy.wait()


def local(
    n,
    ntp,
    queries,
    key_vectors,
    value_vectors,
    attention_out,
    grad_attention,
    mix_input,
    grad_mix,
    input_map,
    output_map,
    decay_log,
):
    tokens, heads, width = queries.shape
    channels = mix_input.shape[1]
    state = input_map.shape[1]
    groups = decay_log.shape[1]
    rows = tokens * heads
    flat = lambda a: a.reshape(-1, width)
    hbm = pl.BlockSpec(memory_space=pltpu.HBM)
    dma = pltpu.SemaphoreType.DMA
    shapes = (
        jax.ShapeDtypeStruct((rows, width), BF16),
        jax.ShapeDtypeStruct((tokens, width), BF16),
        jax.ShapeDtypeStruct((tokens, width), BF16),
        jax.ShapeDtypeStruct((tokens, channels), BF16),
        jax.ShapeDtypeStruct((state, tokens), F32),
        jax.ShapeDtypeStruct((state, tokens), F32),
        jax.ShapeDtypeStruct((groups, tokens), F32),
    )
    outs = pl.pallas_call(
        functools.partial(kernel, n, ntp, heads),
        out_shape=shapes,
        in_specs=[hbm] * 10,
        out_specs=(hbm,) * 7,
        scratch_shapes=[pltpu.VMEM(out.shape, out.dtype) for out in shapes]
        + [
            pltpu.VMEM((rows, width), BF16),
            pltpu.VMEM((rows, width), BF16),
            pltpu.VMEM((rows, width), BF16),
            pltpu.VMEM((tokens, channels), BF16),
            pltpu.VMEM((tokens, channels), BF16),
            pltpu.VMEM((state, tokens), F32),
            pltpu.VMEM((state, tokens), F32),
            pltpu.VMEM((groups, tokens), F32),
            pltpu.VMEM((n, 2 * tokens, width), BF16),
            pltpu.VMEM((n, state, channels), BF16),
            pltpu.VMEM((2, state, channels), BF16),
            pltpu.VMEM((n, 8, 128), F32),
            pltpu.VMEM((n, 2 * tokens, width), BF16),
            pltpu.VMEM((n, 2 * tokens, width), BF16),
            pltpu.VMEM((n // 2, 2 * tokens, width), BF16),
            pltpu.VMEM((n // 2, 2 * tokens, width), F32),
            pltpu.VMEM((ntp, 2 * state, tokens), F32),
            pltpu.VMEM((tokens + 2 * state, channels), BF16),
            pltpu.VMEM((tokens + 2 * state, channels), BF16),
            pltpu.VMEM((state, channels), F32),
            pltpu.VMEM((tokens, channels), F32),
            pltpu.VMEM((tokens, channels), F32),
            pltpu.VMEM((state, channels), F32),
            pltpu.VMEM((n, channels), F32),
            pltpu.VMEM((tokens, channels), F32),
            pltpu.VMEM((tokens, channels), F32),
            pltpu.VMEM((2 * state, tokens), F32),
            pltpu.VMEM((8, rows), F32),
            pltpu.VMEM((8, rows), F32),
            pltpu.VMEM((8, rows), F32),
            pltpu.VMEM((width, rows), F32),
            dma((10,)),
            dma((7,)),
            dma((n,)),
            dma((n,)),
            dma((n,)),
            dma((n,)),
            dma((n,)),
            dma((n,)),
            dma((n,)),
            dma((n,)),
            dma((n,)),
            dma((n,)),
            dma((n // 2,)),
            dma((ntp,)),
            dma((ntp,)),
        ],
        compiler_params=pltpu.CompilerParams(
            collective_id=0, has_side_effects=True, vmem_limit_bytes=63 * 1024 * 1024
        ),
        name="layer_grads",
    )(
        flat(queries),
        flat(key_vectors),
        flat(value_vectors),
        flat(attention_out),
        flat(grad_attention),
        mix_input,
        grad_mix,
        input_map.T,
        output_map.T,
        decay_log.T,
    )
    outs = pl.pallas_call(
        write_out,
        out_shape=shapes,
        in_specs=[hbm] * 7,
        out_specs=(hbm,) * 7,
        compiler_params=pltpu.CompilerParams(vmem_limit_bytes=63 * 1024 * 1024),
        scratch_shapes=[pltpu.VMEM(out.shape, out.dtype) for out in shapes] + [dma((2, 7))],
        name="write_out",
    )(*outs)
    return (
        outs[0].reshape(queries.shape),
        outs[1].reshape(key_vectors.shape),
        outs[2].reshape(value_vectors.shape),
        outs[3], outs[4].T, outs[5].T, outs[6].T)


def solution(mesh):
    seq = P("ctx", "tp", None)
    both = P("ctx", "tp")
    ctx = P("ctx", None)
    return jax.shard_map(
        functools.partial(local, mesh.shape["ctx"], mesh.shape["tp"]),
        mesh=mesh,
        in_specs=(seq, seq, seq, seq, seq, both, both, ctx, ctx, both),
        out_specs=(seq, seq, seq, both, ctx, ctx, both),
        check_vma=False,
    )
```

```python
import functools
import math

import jax
import jax.numpy as jnp
from jax import lax
from jax.experimental import pallas as pl
from jax.experimental.pallas import tpu as pltpu
from jax.sharding import PartitionSpec as P

F32 = jnp.float32
BF16 = jnp.bfloat16
MESH = pl.DeviceIdType.MESH
LOG2E = math.log2(math.e)
MASKED = -1e30


def mm(a, b):
    return lax.dot_general(a, b, (((1,), (0,)), ((), ())), preferred_element_type=F32)


def mm_nt(a, b):
    return lax.dot_general(a, b, (((1,), (1,)), ((), ())), preferred_element_type=F32)


def mm_full(a, b):
    return lax.dot_general(
        a, b, (((1,), (0,)), ((), ())), precision=lax.Precision.HIGHEST, preferred_element_type=F32
    )


def halves(a):
    high = a.astype(BF16)
    return high, (a - high.astype(F32)).astype(BF16)


def mm_split(a, b):
    high, low = halves(a)
    return mm(high, b) + mm(low, b)


def mm_nt_split(a, b):
    high, low = halves(a)
    return mm_nt(high, b) + mm_nt(low, b)


def kernel(
    n,
    ntp,
    heads,
    q_hbm,
    k_hbm,
    v_hbm,
    o_hbm,
    go_hbm,
    x_hbm,
    g_hbm,
    bm_hbm,
    cm_hbm,
    dl_hbm,
    gq_hbm,
    gk_hbm,
    gv_hbm,
    gx_hbm,
    gb_hbm,
    gc_hbm,
    gd_hbm,
    gq_ref,
    gk_ref,
    gv_ref,
    gx_ref,
    gb_ref,
    gc_ref,
    gd_ref,
    q_ref,
    o_ref,
    go_ref,
    x_ref,
    g_ref,
    bm_ref,
    cm_ref,
    dl_ref,
    kv,
    st_out,
    pair_in,
    level_out,
    level_in,
    back_out,
    back_in,
    own_half,
    pair_decay,
    tot,
    grad_out,
    grad_in,
    grad_mid,
    grad_own,
    tp_buf,
    gs,
    xs,
    ends_pre,
    e_wide,
    f_wide,
    half_wide,
    carry_wide,
    out_own,
    in_own,
    maps_own,
    dots_row,
    stat_max,
    stat_sum,
    gq_t,
    load_s,
    store_s,
    kv_s,
    kv_r,
    kv_f,
    st_s,
    st_r,
    st_f,
    tt_s,
    tt_r,
    gr_s,
    gr_r,
    gm_r,
    tp_s,
    tp_r,
):
    me = lax.axis_index("ctx")
    me_tp = lax.axis_index("tp")
    tokens, channels = x_ref.shape
    groups = dl_ref.shape[0]
    state = bm_ref.shape[0]
    column = lax.rem(me, 2)
    level = me // 2
    levels = n // 2
    partner = me + 1 - 2 * column
    rows, width = q_ref.shape
    chunk = 256
    score_scale = 1.0 / math.sqrt(width)

    loads = [
        pltpu.make_async_copy(src, dst, load_s.at[at])
        for at, (src, dst) in enumerate(
            (
                (k_hbm, kv.at[me, pl.ds(0, tokens), :]),
                (v_hbm, kv.at[me, pl.ds(tokens, tokens), :]),
                (dl_hbm, dl_ref),
                (bm_hbm, bm_ref),
                (cm_hbm, cm_ref),
                (g_hbm, g_ref),
                (x_hbm, x_ref),
                (q_hbm, q_ref),
                (go_hbm, go_ref),
                (o_hbm, o_ref),
            )
        )
    ]
    for load in loads:
        load.start()

    stores = [
        pltpu.make_async_copy(src, dst, store_s.at[at])
        for at, (src, dst) in enumerate(
            (
                (gq_ref, gq_hbm),
                (gk_ref, gk_hbm),
                (gv_ref, gv_hbm),
                (gx_ref, gx_hbm),
                (gb_ref, gb_hbm),
                (gc_ref, gc_hbm),
                (gd_ref, gd_hbm),
            )
        )
    ]

    barrier = pltpu.get_barrier_semaphore()

    def greet_ctx(d, c):
        pl.semaphore_signal(
            barrier, inc=1, device_id={"ctx": lax.rem(me + d, n)}, device_id_type=MESH
        )
        return c

    def greet_tp(d, c):
        pl.semaphore_signal(
            barrier, inc=1, device_id={"tp": lax.rem(me_tp + d, ntp)}, device_id_type=MESH
        )
        return c

    lax.fori_loop(1, n, greet_ctx, 0)
    lax.fori_loop(1, ntp, greet_tp, 0)
    loads[0].wait()
    loads[1].wait()
    pl.semaphore_wait(barrier, n - 1 + ntp - 1)

    def kv_copy(src, dst):
        return pltpu.make_async_remote_copy(
            src_ref=kv.at[src],
            dst_ref=kv.at[src],
            send_sem=kv_s.at[dst],
            recv_sem=kv_r.at[src],
            device_id={"ctx": dst},
            device_id_type=MESH,
        )

    def kv_forward(src):
        return pltpu.make_async_remote_copy(
            src_ref=kv.at[src],
            dst_ref=kv.at[src],
            send_sem=kv_f.at[src],
            recv_sem=kv_r.at[src],
            device_id={"ctx": partner},
            device_id_type=MESH,
        )

    def pair_copy():
        return pltpu.make_async_remote_copy(
            src_ref=st_out.at[1 - column],
            dst_ref=pair_in,
            send_sem=st_f.at[0],
            recv_sem=st_f.at[1],
            device_id={"ctx": partner},
            device_id_type=MESH,
        )

    def back_copy():
        return pltpu.make_async_remote_copy(
            src_ref=back_out,
            dst_ref=back_in,
            send_sem=st_f.at[2],
            recv_sem=st_f.at[3],
            device_id={"ctx": partner},
            device_id_type=MESH,
        )

    def level_copy(src, dst, which):
        return pltpu.make_async_remote_copy(
            src_ref=level_out.at[which],
            dst_ref=level_in.at[src // 2],
            send_sem=st_s.at[dst],
            recv_sem=st_r.at[src],
            device_id={"ctx": dst},
            device_id_type=MESH,
        )

    def tot_copy(src, dst):
        return pltpu.make_async_remote_copy(
            src_ref=tot.at[src],
            dst_ref=tot.at[src],
            send_sem=tt_s.at[dst],
            recv_sem=tt_r.at[src],
            device_id={"ctx": dst},
            device_id_type=MESH,
        )

    def grad_copy(src, dst):
        return pltpu.make_async_remote_copy(
            src_ref=grad_out.at[dst],
            dst_ref=grad_in.at[src],
            send_sem=gr_s.at[dst],
            recv_sem=gr_r.at[src],
            device_id={"ctx": dst},
            device_id_type=MESH,
        )

    def grad_pair(dst):
        return pltpu.make_async_remote_copy(
            src_ref=grad_out.at[dst],
            dst_ref=grad_mid.at[dst // 2],
            send_sem=gr_s.at[dst],
            recv_sem=gm_r.at[dst // 2],
            device_id={"ctx": partner},
            device_id_type=MESH,
        )

    def tp_copy(src, dst):
        return pltpu.make_async_remote_copy(
            src_ref=tp_buf.at[src],
            dst_ref=tp_buf.at[src],
            send_sem=tp_s.at[dst],
            recv_sem=tp_r.at[src],
            device_id={"tp": dst},
            device_id_type=MESH,
        )

    @pl.when(column == 0)
    def _():
        kv_copy(me, partner).start()

    def send_kv(d, c):
        kv_copy(me, 2 * (levels - 1 - d) + column).start()
        return c

    lax.fori_loop(0, levels - 1 - level, send_kv, 0)
    for load in loads[2:]:
        load.wait()

    token_row = lax.broadcasted_iota(jnp.int32, (tokens, tokens), 0)
    token_col = lax.broadcasted_iota(jnp.int32, (tokens, tokens), 1)
    lower = token_row >= token_col
    seg = (
        lax.broadcasted_iota(jnp.int32, (groups, channels), 1) // (channels // groups)
        == lax.broadcasted_iota(jnp.int32, (groups, channels), 0)
    ).astype(F32).astype(BF16)

    def tall(wide):
        pad = jnp.zeros((128 - wide.shape[0], tokens), F32)
        return jnp.concatenate([wide, pad], axis=0).T[:, 0 : wide.shape[0]]

    cum = mm_full(lower.astype(F32), tall(dl_ref[...]))
    total = cum[tokens - 1 : tokens, :]
    mid = 0.5 * total
    e_wide[...] = mm_split(jnp.exp(cum - mid), seg)
    f_wide[...] = mm_split(jnp.exp(mid - cum), seg)
    half_wide[...] = mm_split(jnp.exp(jnp.broadcast_to(mid, (state, groups))), seg)
    gs[0:tokens, :] = (e_wide[...] * g_ref[...].astype(F32)).astype(BF16)
    xs[0:tokens, :] = (f_wide[...] * x_ref[...].astype(F32)).astype(BF16)
    in_map_t = bm_ref[...]
    out_map_t = cm_ref[...]
    maps = tall(jnp.concatenate([in_map_t, out_map_t], axis=0))
    in_map = maps[:, 0:state]
    out_map = maps[:, state : 2 * state]
    ends_pre[...] = mm_split(in_map_t, xs[0:tokens, :])
    ends = half_wide[...] * ends_pre[...]
    pulls = half_wide[...] * mm_split(out_map_t, gs[0:tokens, :])
    half = channels // 2
    for side in range(2):
        st_out[side, 0] = ends[:, side * half : (side + 1) * half]
        st_out[side, 1] = pulls[:, side * half : (side + 1) * half]
    tot[me] = jnp.broadcast_to(
        jnp.concatenate([total, jnp.zeros((1, 128 - groups), F32)], axis=1), (8, 128)
    )

    def send_tot(d, c):
        tot_copy(me, lax.rem(me + d, n)).start()
        return c

    pair_copy().start()
    lax.fori_loop(1, n, send_tot, 0)

    key_at = lax.broadcasted_iota(jnp.int32, (tokens, chunk), 0)
    pair_at = lax.broadcasted_iota(jnp.int32, (tokens, chunk), 1)
    ones_row = jnp.ones((8, width), BF16)

    for first in range(0, rows, chunk):
        part = pl.ds(first, chunk)
        prod = go_ref[part, :].astype(F32) * o_ref[part, :].astype(F32)
        high, low = halves(prod)
        dots_row[:, part] = mm_nt(ones_row, high) + mm_nt(ones_row, low)

    def scores_of(keys, first, diagonal):
        scores = mm_nt(keys, q_ref[pl.ds(first, chunk), :]) * (score_scale * LOG2E)
        if diagonal:
            scores = jnp.where(key_at <= (pair_at + first) // heads, scores, MASKED)
        return scores

    own_keys = kv[me, 0:tokens, :]
    for first in range(0, rows, chunk):
        part = pl.ds(first, chunk)
        scores = scores_of(own_keys, first, True)
        top = jnp.max(scores, axis=0, keepdims=True)
        stat_max[:, part] = jnp.broadcast_to(top, (8, chunk))
        stat_sum[:, part] = jnp.broadcast_to(
            jnp.sum(jnp.exp2(scores - top), axis=0, keepdims=True), (8, chunk)
        )

    kernel_sum = jnp.where(lower, mm_nt(gs[0:tokens, :], xs[0:tokens, :]), 0.0)
    maps_own[0:state, :] = mm_full(out_map_t, kernel_sum)
    maps_own[state : 2 * state, :] = mm_full(in_map_t, kernel_sum.T)
    map_dots = jnp.where(lower, mm_full(out_map, in_map_t), 0.0)
    out_own[...] = mm_split(map_dots, xs[0:tokens, :])
    in_own[...] = mm_split(map_dots.T, gs[0:tokens, :])

    def half_seg():
        shape = (groups, half)
        lane = lax.broadcasted_iota(jnp.int32, shape, 1) + column * half
        match = lane // (channels // groups) == lax.broadcasted_iota(jnp.int32, shape, 0)
        return match.astype(F32).astype(BF16)

    is_first = column == 0

    def in_order(mine, theirs):
        return jnp.where(is_first, mine, theirs), jnp.where(is_first, theirs, mine)

    def decay_of(device):
        logs = jnp.broadcast_to(tot[device][0:1, 0:groups], (state, groups))
        return mm_split(jnp.exp(logs), half_seg())

    tot_copy(partner, me).wait_recv()
    pair_copy().wait_recv()
    decay_0, decay_1 = in_order(decay_of(me), decay_of(partner))
    pair_decay[0] = decay_0
    pair_decay[1] = decay_1
    ends_0, ends_1 = in_order(st_out[column, 0], pair_in[0])
    pulls_0, pulls_1 = in_order(st_out[column, 1], pair_in[1])
    level_out[0] = (decay_1 * ends_0 + ends_1).astype(BF16)
    level_out[1] = (pulls_0 + decay_0 * pulls_1).astype(BF16)

    def send_ends(d, c):
        level_copy(me, 2 * (levels - 1 - d) + column, 0).start()
        return c

    def send_pulls(at, c):
        level_copy(me, 2 * at + column, 1).start()
        return c

    lax.fori_loop(0, levels - 1 - level, send_ends, 0)
    lax.fori_loop(0, level, send_pulls, 0)

    def return_states():
        def wait_tot(d, c):
            src = lax.rem(me + d, n)

            @pl.when(src != partner)
            def _():
                tot_copy(src, me).wait_recv()

            return c

        lax.fori_loop(1, n, wait_tot, 0)
        source = lax.broadcasted_iota(jnp.int32, (levels, n), 0)
        passed = lax.broadcasted_iota(jnp.int32, (levels, n), 1) // 2
        between = ((source < passed) & (passed < level)) | ((level < passed) & (passed < source))
        carry_log = mm_full(between.astype(F32), tot[:, 0, :])[:, 0:groups]
        carry_wide[...] = mm_split(jnp.exp(carry_log), half_seg())

        def take_level(at, summed):
            level_copy(2 * at + column, me, 0).wait_recv()
            return summed + carry_wide[pl.ds(at, 1), :] * level_in[at].astype(F32)

        nothing = jnp.zeros((state, half), F32)
        before = lax.fori_loop(0, level, take_level, nothing)
        after = lax.fori_loop(level + 1, levels, take_level, nothing)
        first_ends = jnp.where(is_first, st_out[column, 0], pair_in[0])
        second_pulls = jnp.where(is_first, pair_in[1], st_out[column, 1])
        state_1 = first_ends + pair_decay[0] * before
        pull_0 = second_pulls + pair_decay[1] * after
        own_half[0] = jnp.where(is_first, before, state_1)
        own_half[1] = jnp.where(is_first, pull_0, after)
        back_out[0] = jnp.where(is_first, state_1, before)
        back_out[1] = jnp.where(is_first, after, pull_0)
        back_copy().start()

    def stats_of(src):
        keys = kv[src, 0:tokens, :]
        for first in range(0, rows, chunk):
            part = pl.ds(first, chunk)
            scores = scores_of(keys, first, False)
            before = stat_max[0:1, part]
            top = jnp.maximum(before, jnp.max(scores, axis=0, keepdims=True))
            summed = stat_sum[0:1, part] * jnp.exp2(before - top) + jnp.sum(
                jnp.exp2(scores - top), axis=0, keepdims=True
            )
            stat_max[:, part] = jnp.broadcast_to(top, (8, chunk))
            stat_sum[:, part] = jnp.broadcast_to(summed, (8, chunk))

    def stats_step(d, c):
        src = 2 * (level - d) + column
        across = 2 * (level - d + 1) + 1 - column
        kv_copy(src, me).wait_recv()
        kv_forward(src).start()
        stats_of(src)

        @pl.when(across < me)
        def _():
            kv_copy(across, me).wait_recv()
            stats_of(across)

        return c

    lax.fori_loop(1, level + 1, stats_step, 0)

    @pl.when(me > 0)
    def _():
        kv_copy(1 - column, me).wait_recv()
        stats_of(1 - column)

    stat_max[...] = stat_max[...] + jnp.log(stat_sum[...]) * LOG2E
    gq_t[...] = jnp.zeros_like(gq_t)

    def grads_of(keys, values, diagonal):
        keys_t = keys.astype(F32).T.astype(BF16)
        key_sum = jnp.zeros((tokens, width), F32)
        value_sum = jnp.zeros((tokens, width), F32)
        for first in range(0, rows, chunk):
            part = pl.ds(first, chunk)
            queries = q_ref[part, :]
            grads = go_ref[part, :]
            probs = jnp.exp2(scores_of(keys, first, diagonal) - stat_max[0:1, part])
            grad_probs = mm_nt(values, grads)
            grad_scores = (probs * (grad_probs - dots_row[0:1, part]) * score_scale).astype(BF16)
            value_sum = value_sum + mm(probs.astype(BF16), grads)
            key_sum = key_sum + mm(grad_scores, queries)
            gq_t[:, part] += mm(keys_t, grad_scores)
        return key_sum, value_sum

    def grads_across(src):
        key_sum, value_sum = grads_of(kv[src, 0:tokens, :], kv[src, tokens : 2 * tokens, :], False)
        grad_out[src, 0:tokens, :] = key_sum.astype(BF16)
        grad_out[src, tokens : 2 * tokens, :] = value_sum.astype(BF16)

    def pass_on(at):
        dst = 2 * at + column
        grad_pair(dst).wait_recv()
        grad_out[dst] = (grad_own[at] + grad_mid[at].astype(F32)).astype(BF16)
        grad_copy(me, dst).start()

    def grads_step(at, c):
        @pl.when(at == level - 1)
        def _():
            return_states()

        across = 2 * at + 1 - column
        grads_across(across)
        grad_pair(across).start()
        src = 2 * at + column
        key_sum, value_sum = grads_of(kv[src, 0:tokens, :], kv[src, tokens : 2 * tokens, :], False)
        grad_own[at, 0:tokens, :] = key_sum
        grad_own[at, tokens : 2 * tokens, :] = value_sum

        @pl.when(at > 0)
        def _():
            pass_on(at - 1)

        return c

    lax.fori_loop(0, level, grads_step, 0)

    @pl.when(level == 0)
    def _():
        return_states()

    @pl.when(column == 1)
    def _():
        grads_across(partner)
        grad_copy(me, partner).start()

    @pl.when(level > 0)
    def _():
        pass_on(level - 1)

    own_key_sum, own_value_sum = grads_of(own_keys, kv[me, tokens : 2 * tokens, :], True)
    gq_ref[...] = gq_t[...].T.astype(BF16)
    stores[0].start()

    back_copy().wait_recv()

    def whole(which):
        sides = in_order(own_half[which], back_in[which])
        return jnp.concatenate(sides, axis=1) * half_wide[...]

    state_in = whole(0)
    pull_in = whole(1)
    for ref, arrived in ((xs, state_in), (gs, pull_in)):
        high, low = halves(arrived)
        ref[tokens : tokens + state, :] = high
        ref[tokens + state : tokens + 2 * state, :] = low
    pulled = mm_nt(gs[tokens : tokens + 2 * state, :], xs[0:tokens, :])
    carried = mm_nt(xs[tokens : tokens + 2 * state, :], gs[0:tokens, :])
    tp_buf[me_tp, 0:state, :] = (
        maps_own[0:state, :] + pulled[0:state] + pulled[state : 2 * state]
    )
    tp_buf[me_tp, state : 2 * state, :] = (
        maps_own[state : 2 * state, :] + carried[0:state] + carried[state : 2 * state]
    )

    def send_tp(d, c):
        tp_copy(me_tp, lax.rem(me_tp + d, ntp)).start()
        return c

    lax.fori_loop(1, ntp, send_tp, 0)

    from_state = jnp.concatenate([out_map, out_map], axis=1)
    from_pull = jnp.concatenate([in_map, in_map], axis=1)
    out_pre = out_own[...] + mm_split(from_state, xs[tokens : tokens + 2 * state, :])
    in_pre = in_own[...] + mm_split(from_pull, gs[tokens : tokens + 2 * state, :])
    gx_ref[...] = (f_wide[...] * in_pre).astype(BF16)
    stores[3].start()
    per_token = gs[0:tokens, :].astype(F32) * out_pre - xs[0:tokens, :].astype(F32) * in_pre
    at_end = pull_in * (state_in + ends_pre[...])
    seg_token = mm_nt_split(per_token, seg)
    seg_end = mm_nt_split(at_end, seg)
    grad_decay = mm_full((token_row <= token_col).astype(F32), seg_token) + jnp.sum(
        seg_end, axis=0, keepdims=True
    )
    gd_ref[...] = jnp.concatenate(
        [grad_decay, jnp.zeros((tokens, 128 - groups), F32)], axis=1
    ).T[0:groups, :]
    stores[6].start()

    @pl.when(column == 0)
    def _():
        grad_copy(partner, me).wait_recv()

    @pl.when(column == 1)
    def _():
        grad_in[partner] = jnp.zeros((2 * tokens, width), BF16)

    def take_grads(at, carry):
        src = 2 * at + column
        grad_copy(src, me).wait_recv()
        return (
            carry[0] + grad_in[src, 0:tokens, :].astype(F32),
            carry[1] + grad_in[src, tokens : 2 * tokens, :].astype(F32),
        )

    key_total, value_total = lax.fori_loop(
        level + 1,
        levels,
        take_grads,
        (
            own_key_sum + grad_in[partner, 0:tokens, :].astype(F32),
            own_value_sum + grad_in[partner, tokens : 2 * tokens, :].astype(F32),
        ),
    )
    gk_ref[...] = key_total.astype(BF16)
    gv_ref[...] = value_total.astype(BF16)
    stores[1].start()
    stores[2].start()

    def wait_tp(d, c):
        tp_copy(lax.rem(me_tp + d, ntp), me_tp).wait_recv()
        return c

    lax.fori_loop(1, ntp, wait_tp, 0)
    map_grads = tp_buf[0]
    for other in range(1, ntp):
        map_grads = map_grads + tp_buf[other]
    gb_ref[...] = map_grads[0:state, :]
    gc_ref[...] = map_grads[state : 2 * state, :]
    stores[4].start()
    stores[5].start()

    def end_tp(d, c):
        tp_copy(me_tp, lax.rem(me_tp + d, ntp)).wait_send()
        return c

    def end_tot(d, c):
        tot_copy(me, lax.rem(me + d, n)).wait_send()
        return c

    def end_states(d, c):
        level_copy(me, lax.rem(me + 2 * d, n), 0).wait_send()
        return c

    def end_kv(at, c):
        kv_copy(me, 2 * at + column).wait_send()
        return c

    def end_kv_forward(at, c):
        kv_forward(2 * at + column).wait_send()
        return c

    def end_grads(dst, c):
        grad_copy(me, dst).wait_send()
        return c

    lax.fori_loop(1, ntp, end_tp, 0)
    lax.fori_loop(1, n, end_tot, 0)
    pair_copy().wait_send()
    back_copy().wait_send()
    lax.fori_loop(1, levels, end_states, 0)

    @pl.when(column == 0)
    def _():
        kv_copy(me, partner).wait_send()

    lax.fori_loop(level + 1, levels, end_kv, 0)
    lax.fori_loop(0, level, end_kv_forward, 0)
    lax.fori_loop(0, me, end_grads, 0)
    for store in stores:
        store.wait()


def write_out(*refs):
    count = len(refs) // 3
    ins, outs, held = refs[:count], refs[count : 2 * count], refs[2 * count : 3 * count]
    sems = refs[-1]
    arrive = [pltpu.make_async_copy(ins[at], held[at], sems.at[0, at]) for at in range(count)]
    leave = [pltpu.make_async_copy(held[at], outs[at], sems.at[1, at]) for at in range(count)]
    for copy in arrive:
        copy.start()
    for at in range(count):
        arrive[at].wait()
        leave[at].start()
    for copy in leave:
        copy.wait()


def local(
    n,
    ntp,
    queries,
    key_vectors,
    value_vectors,
    attention_out,
    grad_attention,
    mix_input,
    grad_mix,
    input_map,
    output_map,
    decay_log,
):
    tokens, heads, width = queries.shape
    channels = mix_input.shape[1]
    state = input_map.shape[1]
    groups = decay_log.shape[1]
    rows = tokens * heads
    flat = lambda a: a.reshape(-1, width)
    hbm = pl.BlockSpec(memory_space=pltpu.HBM)
    dma = pltpu.SemaphoreType.DMA
    shapes = (
        jax.ShapeDtypeStruct((rows, width), BF16),
        jax.ShapeDtypeStruct((tokens, width), BF16),
        jax.ShapeDtypeStruct((tokens, width), BF16),
        jax.ShapeDtypeStruct((tokens, channels), BF16),
        jax.ShapeDtypeStruct((state, tokens), F32),
        jax.ShapeDtypeStruct((state, tokens), F32),
        jax.ShapeDtypeStruct((groups, tokens), F32),
    )
    outs = pl.pallas_call(
        functools.partial(kernel, n, ntp, heads),
        out_shape=shapes,
        in_specs=[hbm] * 10,
        out_specs=(hbm,) * 7,
        scratch_shapes=[pltpu.VMEM(out.shape, out.dtype) for out in shapes]
        + [
            pltpu.VMEM((rows, width), BF16),
            pltpu.VMEM((rows, width), BF16),
            pltpu.VMEM((rows, width), BF16),
            pltpu.VMEM((tokens, channels), BF16),
            pltpu.VMEM((tokens, channels), BF16),
            pltpu.VMEM((state, tokens), F32),
            pltpu.VMEM((state, tokens), F32),
            pltpu.VMEM((groups, tokens), F32),
            pltpu.VMEM((n, 2 * tokens, width), BF16),
            pltpu.VMEM((2, 2, state, channels // 2), F32),
            pltpu.VMEM((2, state, channels // 2), F32),
            pltpu.VMEM((2, state, channels // 2), BF16),
            pltpu.VMEM((n // 2, state, channels // 2), BF16),
            pltpu.VMEM((2, state, channels // 2), F32),
            pltpu.VMEM((2, state, channels // 2), F32),
            pltpu.VMEM((2, state, channels // 2), F32),
            pltpu.VMEM((2, state, channels // 2), F32),
            pltpu.VMEM((n, 8, 128), F32),
            pltpu.VMEM((n, 2 * tokens, width), BF16),
            pltpu.VMEM((n, 2 * tokens, width), BF16),
            pltpu.VMEM((n // 2, 2 * tokens, width), BF16),
            pltpu.VMEM((n // 2, 2 * tokens, width), F32),
            pltpu.VMEM((ntp, 2 * state, tokens), F32),
            pltpu.VMEM((tokens + 2 * state, channels), BF16),
            pltpu.VMEM((tokens + 2 * state, channels), BF16),
            pltpu.VMEM((state, channels), F32),
            pltpu.VMEM((tokens, channels), F32),
            pltpu.VMEM((tokens, channels), F32),
            pltpu.VMEM((state, channels), F32),
            pltpu.VMEM((n // 2, channels // 2), F32),
            pltpu.VMEM((tokens, channels), F32),
            pltpu.VMEM((tokens, channels), F32),
            pltpu.VMEM((2 * state, tokens), F32),
            pltpu.VMEM((8, rows), F32),
            pltpu.VMEM((8, rows), F32),
            pltpu.VMEM((8, rows), F32),
            pltpu.VMEM((width, rows), F32),
            dma((10,)),
            dma((7,)),
            dma((n,)),
            dma((n,)),
            dma((n,)),
            dma((n,)),
            dma((n,)),
            dma((n,)),
            dma((n,)),
            dma((n,)),
            dma((n,)),
            dma((n,)),
            dma((n // 2,)),
            dma((ntp,)),
            dma((ntp,)),
        ],
        compiler_params=pltpu.CompilerParams(
            collective_id=0, has_side_effects=True, vmem_limit_bytes=63 * 1024 * 1024
        ),
        name="layer_grads",
    )(
        flat(queries),
        flat(key_vectors),
        flat(value_vectors),
        flat(attention_out),
        flat(grad_attention),
        mix_input,
        grad_mix,
        input_map.T,
        output_map.T,
        decay_log.T,
    )
    outs = pl.pallas_call(
        write_out,
        out_shape=shapes,
        in_specs=[hbm] * 7,
        out_specs=(hbm,) * 7,
        compiler_params=pltpu.CompilerParams(vmem_limit_bytes=63 * 1024 * 1024),
        scratch_shapes=[pltpu.VMEM(out.shape, out.dtype) for out in shapes] + [dma((2, 7))],
        name="write_out",
    )(*outs)
    return (
        outs[0].reshape(queries.shape),
        outs[1].reshape(key_vectors.shape),
        outs[2].reshape(value_vectors.shape),
        outs[3], outs[4].T, outs[5].T, outs[6].T)


def solution(mesh):
    seq = P("ctx", "tp", None)
    both = P("ctx", "tp")
    ctx = P("ctx", None)
    return jax.shard_map(
        functools.partial(local, mesh.shape["ctx"], mesh.shape["tp"]),
        mesh=mesh,
        in_specs=(seq, seq, seq, seq, seq, both, both, ctx, ctx, both),
        out_specs=(seq, seq, seq, both, ctx, ctx, both),
        check_vma=False,
    )
```

```python
import functools
import math

import jax
import jax.numpy as jnp
from jax import lax
from jax.experimental import pallas as pl
from jax.experimental.pallas import tpu as pltpu
from jax.sharding import PartitionSpec as P

F32 = jnp.float32
BF16 = jnp.bfloat16
MESH = pl.DeviceIdType.MESH
LOG2E = math.log2(math.e)
MASKED = -1e30


def mm(a, b):
    return lax.dot_general(a, b, (((1,), (0,)), ((), ())), preferred_element_type=F32)


def mm_nt(a, b):
    return lax.dot_general(a, b, (((1,), (1,)), ((), ())), preferred_element_type=F32)


def mm_full(a, b):
    return lax.dot_general(
        a, b, (((1,), (0,)), ((), ())), precision=lax.Precision.HIGHEST, preferred_element_type=F32
    )


def halves(a):
    high = a.astype(BF16)
    return high, (a - high.astype(F32)).astype(BF16)


def mm_split(a, b):
    high, low = halves(a)
    return mm(high, b) + mm(low, b)


def mm_nt_split(a, b):
    high, low = halves(a)
    return mm_nt(high, b) + mm_nt(low, b)


def kernel(
    n,
    ntp,
    heads,
    q_hbm,
    k_hbm,
    v_hbm,
    o_hbm,
    go_hbm,
    x_hbm,
    g_hbm,
    bm_hbm,
    cm_hbm,
    dl_hbm,
    gq_hbm,
    gk_hbm,
    gv_hbm,
    gx_hbm,
    gb_hbm,
    gc_hbm,
    gd_hbm,
    gq_ref,
    gk_ref,
    gv_ref,
    gx_ref,
    gb_ref,
    gc_ref,
    gd_ref,
    q_ref,
    o_ref,
    go_ref,
    x_ref,
    g_ref,
    bm_ref,
    cm_ref,
    dl_ref,
    kv,
    st_out,
    pair_in,
    level_out,
    level_in,
    back_out,
    back_in,
    own_half,
    pair_decay,
    tot,
    grad_out,
    grad_in,
    grad_mid,
    grad_own,
    tp_buf,
    gs,
    xs,
    ends_pre,
    e_wide,
    f_wide,
    half_wide,
    carry_wide,
    out_own,
    in_own,
    maps_own,
    dots_row,
    stat_max,
    stat_sum,
    gq_t,
    load_s,
    store_s,
    kv_s,
    kv_r,
    kv_f,
    st_s,
    st_r,
    st_f,
    tt_s,
    tt_r,
    gr_s,
    gr_r,
    gm_r,
    tp_s,
    tp_r,
):
    me = lax.axis_index("ctx")
    me_tp = lax.axis_index("tp")
    tokens, channels = x_ref.shape
    groups = dl_ref.shape[0]
    state = bm_ref.shape[0]
    column = lax.rem(me, 2)
    level = me // 2
    levels = n // 2
    partner = me + 1 - 2 * column
    rows, width = q_ref.shape
    chunk = 256
    score_scale = 1.0 / math.sqrt(width)

    loads = [
        pltpu.make_async_copy(src, dst, load_s.at[at])
        for at, (src, dst) in enumerate(
            (
                (k_hbm, kv.at[me, pl.ds(0, tokens), :]),
                (v_hbm, kv.at[me, pl.ds(tokens, tokens), :]),
                (dl_hbm, dl_ref),
                (bm_hbm, bm_ref),
                (cm_hbm, cm_ref),
                (g_hbm, g_ref),
                (x_hbm, x_ref),
                (q_hbm, q_ref),
                (go_hbm, go_ref),
                (o_hbm, o_ref),
            )
        )
    ]
    for load in loads:
        load.start()

    stores = [
        pltpu.make_async_copy(src, dst, store_s.at[at])
        for at, (src, dst) in enumerate(
            (
                (gq_ref, gq_hbm),
                (gk_ref, gk_hbm),
                (gv_ref, gv_hbm),
                (gx_ref, gx_hbm),
                (gb_ref, gb_hbm),
                (gc_ref, gc_hbm),
                (gd_ref, gd_hbm),
            )
        )
    ]

    barrier = pltpu.get_barrier_semaphore()

    def greet_ctx(d, c):
        pl.semaphore_signal(
            barrier, inc=1, device_id={"ctx": lax.rem(me + d, n)}, device_id_type=MESH
        )
        return c

    def greet_tp(d, c):
        pl.semaphore_signal(
            barrier, inc=1, device_id={"tp": lax.rem(me_tp + d, ntp)}, device_id_type=MESH
        )
        return c

    lax.fori_loop(1, n, greet_ctx, 0)
    lax.fori_loop(1, ntp, greet_tp, 0)
    loads[0].wait()
    loads[1].wait()
    pl.semaphore_wait(barrier, n - 1 + ntp - 1)

    def kv_copy(src, dst):
        return pltpu.make_async_remote_copy(
            src_ref=kv.at[src],
            dst_ref=kv.at[src],
            send_sem=kv_s.at[dst],
            recv_sem=kv_r.at[src],
            device_id={"ctx": dst},
            device_id_type=MESH,
        )

    def kv_forward(src):
        return pltpu.make_async_remote_copy(
            src_ref=kv.at[src],
            dst_ref=kv.at[src],
            send_sem=kv_f.at[src],
            recv_sem=kv_r.at[src],
            device_id={"ctx": partner},
            device_id_type=MESH,
        )

    def pair_copy():
        return pltpu.make_async_remote_copy(
            src_ref=st_out.at[1 - column],
            dst_ref=pair_in,
            send_sem=st_f.at[0],
            recv_sem=st_f.at[1],
            device_id={"ctx": partner},
            device_id_type=MESH,
        )

    def back_copy():
        return pltpu.make_async_remote_copy(
            src_ref=back_out,
            dst_ref=back_in,
            send_sem=st_f.at[2],
            recv_sem=st_f.at[3],
            device_id={"ctx": partner},
            device_id_type=MESH,
        )

    def level_copy(src, dst, which):
        return pltpu.make_async_remote_copy(
            src_ref=level_out.at[which],
            dst_ref=level_in.at[src // 2],
            send_sem=st_s.at[dst],
            recv_sem=st_r.at[src],
            device_id={"ctx": dst},
            device_id_type=MESH,
        )

    def tot_copy(src, dst):
        return pltpu.make_async_remote_copy(
            src_ref=tot.at[src],
            dst_ref=tot.at[src],
            send_sem=tt_s.at[dst],
            recv_sem=tt_r.at[src],
            device_id={"ctx": dst},
            device_id_type=MESH,
        )

    def grad_copy(src, dst):
        return pltpu.make_async_remote_copy(
            src_ref=grad_out.at[dst],
            dst_ref=grad_in.at[src],
            send_sem=gr_s.at[dst],
            recv_sem=gr_r.at[src],
            device_id={"ctx": dst},
            device_id_type=MESH,
        )

    def grad_pair(dst):
        return pltpu.make_async_remote_copy(
            src_ref=grad_out.at[dst],
            dst_ref=grad_mid.at[dst // 2],
            send_sem=gr_s.at[dst],
            recv_sem=gm_r.at[dst // 2],
            device_id={"ctx": partner},
            device_id_type=MESH,
        )

    def tp_copy(src, dst):
        return pltpu.make_async_remote_copy(
            src_ref=tp_buf.at[src],
            dst_ref=tp_buf.at[src],
            send_sem=tp_s.at[dst],
            recv_sem=tp_r.at[src],
            device_id={"tp": dst},
            device_id_type=MESH,
        )

    @pl.when(column == 0)
    def _():
        kv_copy(me, partner).start()

    def send_kv(d, c):
        kv_copy(me, 2 * (levels - 1 - d) + column).start()
        return c

    lax.fori_loop(0, levels - 1 - level, send_kv, 0)
    for load in loads[2:]:
        load.wait()

    token_row = lax.broadcasted_iota(jnp.int32, (tokens, tokens), 0)
    token_col = lax.broadcasted_iota(jnp.int32, (tokens, tokens), 1)
    lower = token_row >= token_col
    seg = (
        lax.broadcasted_iota(jnp.int32, (groups, channels), 1) // (channels // groups)
        == lax.broadcasted_iota(jnp.int32, (groups, channels), 0)
    ).astype(F32).astype(BF16)

    def tall(wide):
        pad = jnp.zeros((128 - wide.shape[0], tokens), F32)
        return jnp.concatenate([wide, pad], axis=0).T[:, 0 : wide.shape[0]]

    cum = mm_full(lower.astype(F32), tall(dl_ref[...]))
    total = cum[tokens - 1 : tokens, :]
    mid = 0.5 * total
    e_wide[...] = mm_split(jnp.exp(cum - mid), seg)
    f_wide[...] = mm_split(jnp.exp(mid - cum), seg)
    half_wide[...] = mm_split(jnp.exp(jnp.broadcast_to(mid, (state, groups))), seg)
    gs[0:tokens, :] = (e_wide[...] * g_ref[...].astype(F32)).astype(BF16)
    xs[0:tokens, :] = (f_wide[...] * x_ref[...].astype(F32)).astype(BF16)
    in_map_t = bm_ref[...]
    out_map_t = cm_ref[...]
    maps = tall(jnp.concatenate([in_map_t, out_map_t], axis=0))
    in_map = maps[:, 0:state]
    out_map = maps[:, state : 2 * state]
    ends_pre[...] = mm_split(in_map_t, xs[0:tokens, :])
    ends = half_wide[...] * ends_pre[...]
    pulls = half_wide[...] * mm_split(out_map_t, gs[0:tokens, :])
    half = channels // 2
    for side in range(2):
        st_out[side, 0] = ends[:, side * half : (side + 1) * half]
        st_out[side, 1] = pulls[:, side * half : (side + 1) * half]
    tot[me] = jnp.broadcast_to(
        jnp.concatenate([total, jnp.zeros((1, 128 - groups), F32)], axis=1), (8, 128)
    )

    def send_tot(d, c):
        tot_copy(me, lax.rem(me + d, n)).start()
        return c

    pair_copy().start()
    lax.fori_loop(1, n, send_tot, 0)

    key_at = lax.broadcasted_iota(jnp.int32, (tokens, chunk), 0)
    pair_at = lax.broadcasted_iota(jnp.int32, (tokens, chunk), 1)
    ones_row = jnp.ones((8, width), BF16)

    for first in range(0, rows, chunk):
        part = pl.ds(first, chunk)
        prod = go_ref[part, :].astype(F32) * o_ref[part, :].astype(F32)
        high, low = halves(prod)
        dots_row[:, part] = mm_nt(ones_row, high) + mm_nt(ones_row, low)

    def scores_of(keys, first, diagonal):
        scores = mm_nt(keys, q_ref[pl.ds(first, chunk), :]) * (score_scale * LOG2E)
        if diagonal:
            scores = jnp.where(key_at <= (pair_at + first) // heads, scores, MASKED)
        return scores

    own_keys = kv[me, 0:tokens, :]
    for first in range(0, rows, chunk):
        part = pl.ds(first, chunk)
        scores = scores_of(own_keys, first, True)
        top = jnp.max(scores, axis=0, keepdims=True)
        stat_max[:, part] = jnp.broadcast_to(top, (8, chunk))
        stat_sum[:, part] = jnp.broadcast_to(
            jnp.sum(jnp.exp2(scores - top), axis=0, keepdims=True), (8, chunk)
        )

    kernel_sum = jnp.where(lower, mm_nt(gs[0:tokens, :], xs[0:tokens, :]), 0.0)
    maps_own[0:state, :] = mm_full(out_map_t, kernel_sum)
    maps_own[state : 2 * state, :] = mm_full(in_map_t, kernel_sum.T)
    map_dots = jnp.where(lower, mm_full(out_map, in_map_t), 0.0)
    out_own[...] = mm_split(map_dots, xs[0:tokens, :])
    in_own[...] = mm_split(map_dots.T, gs[0:tokens, :])

    def half_seg():
        shape = (groups, half)
        lane = lax.broadcasted_iota(jnp.int32, shape, 1) + column * half
        match = lane // (channels // groups) == lax.broadcasted_iota(jnp.int32, shape, 0)
        return match.astype(F32).astype(BF16)

    is_first = column == 0

    def in_order(mine, theirs):
        return jnp.where(is_first, mine, theirs), jnp.where(is_first, theirs, mine)

    def decay_of(device):
        logs = jnp.broadcast_to(tot[device][0:1, 0:groups], (state, groups))
        return mm_split(jnp.exp(logs), half_seg())

    tot_copy(partner, me).wait_recv()
    pair_copy().wait_recv()
    decay_0, decay_1 = in_order(decay_of(me), decay_of(partner))
    pair_decay[0] = decay_0
    pair_decay[1] = decay_1
    ends_0, ends_1 = in_order(st_out[column, 0], pair_in[0])
    pulls_0, pulls_1 = in_order(st_out[column, 1], pair_in[1])
    level_out[0] = (decay_1 * ends_0 + ends_1).astype(BF16)
    level_out[1] = (pulls_0 + decay_0 * pulls_1).astype(BF16)

    def send_ends(d, c):
        level_copy(me, 2 * (levels - 1 - d) + column, 0).start()
        return c

    def send_pulls(at, c):
        level_copy(me, 2 * at + column, 1).start()
        return c

    lax.fori_loop(0, levels - 1 - level, send_ends, 0)
    lax.fori_loop(0, level, send_pulls, 0)

    def return_states():
        def wait_tot(d, c):
            src = lax.rem(me + d, n)

            @pl.when(src != partner)
            def _():
                tot_copy(src, me).wait_recv()

            return c

        lax.fori_loop(1, n, wait_tot, 0)
        source = lax.broadcasted_iota(jnp.int32, (levels, n), 0)
        passed = lax.broadcasted_iota(jnp.int32, (levels, n), 1) // 2
        between = ((source < passed) & (passed < level)) | ((level < passed) & (passed < source))
        carry_log = mm_full(between.astype(F32), tot[:, 0, :])[:, 0:groups]
        carry_wide[...] = mm_split(jnp.exp(carry_log), half_seg())

        def take_level(at, summed):
            level_copy(2 * at + column, me, 0).wait_recv()
            return summed + carry_wide[pl.ds(at, 1), :] * level_in[at].astype(F32)

        nothing = jnp.zeros((state, half), F32)
        before = lax.fori_loop(0, level, take_level, nothing)
        after = lax.fori_loop(level + 1, levels, take_level, nothing)
        first_ends = jnp.where(is_first, st_out[column, 0], pair_in[0])
        second_pulls = jnp.where(is_first, pair_in[1], st_out[column, 1])
        state_1 = first_ends + pair_decay[0] * before
        pull_0 = second_pulls + pair_decay[1] * after
        own_half[0] = jnp.where(is_first, before, state_1)
        own_half[1] = jnp.where(is_first, pull_0, after)
        back_out[0] = jnp.where(is_first, state_1, before)
        back_out[1] = jnp.where(is_first, after, pull_0)
        back_copy().start()

    def stats_of(src):
        keys = kv[src, 0:tokens, :]
        for first in range(0, rows, chunk):
            part = pl.ds(first, chunk)
            scores = scores_of(keys, first, False)
            before = stat_max[0:1, part]
            top = jnp.maximum(before, jnp.max(scores, axis=0, keepdims=True))
            summed = stat_sum[0:1, part] * jnp.exp2(before - top) + jnp.sum(
                jnp.exp2(scores - top), axis=0, keepdims=True
            )
            stat_max[:, part] = jnp.broadcast_to(top, (8, chunk))
            stat_sum[:, part] = jnp.broadcast_to(summed, (8, chunk))

    def stats_step(d, c):
        src = 2 * (level - d) + column
        across = 2 * (level - d + 1) + 1 - column
        stats_of(src)

        @pl.when(across < me)
        def _():
            kv_copy(across, me).wait_recv()
            stats_of(across)

        return c

    def forward_kv(d, c):
        src = 2 * (level - d) + column
        kv_copy(src, me).wait_recv()
        kv_forward(src).start()
        return c

    lax.fori_loop(1, level + 1, forward_kv, 0)
    lax.fori_loop(1, level + 1, stats_step, 0)

    @pl.when(me > 0)
    def _():
        kv_copy(1 - column, me).wait_recv()
        stats_of(1 - column)

    stat_max[...] = stat_max[...] + jnp.log(stat_sum[...]) * LOG2E
    gq_t[...] = jnp.zeros_like(gq_t)

    def grads_of(keys, values, diagonal):
        keys_t = keys.astype(F32).T.astype(BF16)
        key_sum = jnp.zeros((tokens, width), F32)
        value_sum = jnp.zeros((tokens, width), F32)
        for first in range(0, rows, chunk):
            part = pl.ds(first, chunk)
            queries = q_ref[part, :]
            grads = go_ref[part, :]
            probs = jnp.exp2(scores_of(keys, first, diagonal) - stat_max[0:1, part])
            grad_probs = mm_nt(values, grads)
            grad_scores = (probs * (grad_probs - dots_row[0:1, part]) * score_scale).astype(BF16)
            value_sum = value_sum + mm(probs.astype(BF16), grads)
            key_sum = key_sum + mm(grad_scores, queries)
            gq_t[:, part] += mm(keys_t, grad_scores)
        return key_sum, value_sum

    def grads_across(src):
        key_sum, value_sum = grads_of(kv[src, 0:tokens, :], kv[src, tokens : 2 * tokens, :], False)
        grad_out[src, 0:tokens, :] = key_sum.astype(BF16)
        grad_out[src, tokens : 2 * tokens, :] = value_sum.astype(BF16)

    def pass_on(at):
        dst = 2 * at + column
        grad_pair(dst).wait_recv()
        grad_out[dst] = (grad_own[at] + grad_mid[at].astype(F32)).astype(BF16)
        grad_copy(me, dst).start()

    def grads_step(at, c):
        @pl.when(at == level - 1)
        def _():
            return_states()

        across = 2 * at + 1 - column
        grads_across(across)
        grad_pair(across).start()
        src = 2 * at + column
        key_sum, value_sum = grads_of(kv[src, 0:tokens, :], kv[src, tokens : 2 * tokens, :], False)
        grad_own[at, 0:tokens, :] = key_sum
        grad_own[at, tokens : 2 * tokens, :] = value_sum

        @pl.when(at > 0)
        def _():
            pass_on(at - 1)

        return c

    lax.fori_loop(0, level, grads_step, 0)

    @pl.when(level == 0)
    def _():
        return_states()

    @pl.when(column == 1)
    def _():
        grads_across(partner)
        grad_copy(me, partner).start()

    @pl.when(level > 0)
    def _():
        pass_on(level - 1)

    own_key_sum, own_value_sum = grads_of(own_keys, kv[me, tokens : 2 * tokens, :], True)
    gq_ref[...] = gq_t[...].T.astype(BF16)
    stores[0].start()

    back_copy().wait_recv()

    def whole(which):
        sides = in_order(own_half[which], back_in[which])
        return jnp.concatenate(sides, axis=1) * half_wide[...]

    state_in = whole(0)
    pull_in = whole(1)
    for ref, arrived in ((xs, state_in), (gs, pull_in)):
        high, low = halves(arrived)
        ref[tokens : tokens + state, :] = high
        ref[tokens + state : tokens + 2 * state, :] = low
    pulled = mm_nt(gs[tokens : tokens + 2 * state, :], xs[0:tokens, :])
    carried = mm_nt(xs[tokens : tokens + 2 * state, :], gs[0:tokens, :])
    tp_buf[me_tp, 0:state, :] = (
        maps_own[0:state, :] + pulled[0:state] + pulled[state : 2 * state]
    )
    tp_buf[me_tp, state : 2 * state, :] = (
        maps_own[state : 2 * state, :] + carried[0:state] + carried[state : 2 * state]
    )

    def send_tp(d, c):
        tp_copy(me_tp, lax.rem(me_tp + d, ntp)).start()
        return c

    lax.fori_loop(1, ntp, send_tp, 0)

    from_state = jnp.concatenate([out_map, out_map], axis=1)
    from_pull = jnp.concatenate([in_map, in_map], axis=1)
    out_pre = out_own[...] + mm_split(from_state, xs[tokens : tokens + 2 * state, :])
    in_pre = in_own[...] + mm_split(from_pull, gs[tokens : tokens + 2 * state, :])
    gx_ref[...] = (f_wide[...] * in_pre).astype(BF16)
    stores[3].start()
    per_token = gs[0:tokens, :].astype(F32) * out_pre - xs[0:tokens, :].astype(F32) * in_pre
    at_end = pull_in * (state_in + ends_pre[...])
    seg_token = mm_nt_split(per_token, seg)
    seg_end = mm_nt_split(at_end, seg)
    grad_decay = mm_full((token_row <= token_col).astype(F32), seg_token) + jnp.sum(
        seg_end, axis=0, keepdims=True
    )
    gd_ref[...] = jnp.concatenate(
        [grad_decay, jnp.zeros((tokens, 128 - groups), F32)], axis=1
    ).T[0:groups, :]
    stores[6].start()

    @pl.when(column == 0)
    def _():
        grad_copy(partner, me).wait_recv()

    @pl.when(column == 1)
    def _():
        grad_in[partner] = jnp.zeros((2 * tokens, width), BF16)

    def take_grads(at, carry):
        src = 2 * at + column
        grad_copy(src, me).wait_recv()
        return (
            carry[0] + grad_in[src, 0:tokens, :].astype(F32),
            carry[1] + grad_in[src, tokens : 2 * tokens, :].astype(F32),
        )

    key_total, value_total = lax.fori_loop(
        level + 1,
        levels,
        take_grads,
        (
            own_key_sum + grad_in[partner, 0:tokens, :].astype(F32),
            own_value_sum + grad_in[partner, tokens : 2 * tokens, :].astype(F32),
        ),
    )
    gk_ref[...] = key_total.astype(BF16)
    gv_ref[...] = value_total.astype(BF16)
    stores[1].start()
    stores[2].start()

    def wait_tp(d, c):
        tp_copy(lax.rem(me_tp + d, ntp), me_tp).wait_recv()
        return c

    lax.fori_loop(1, ntp, wait_tp, 0)
    map_grads = tp_buf[0]
    for other in range(1, ntp):
        map_grads = map_grads + tp_buf[other]
    gb_ref[...] = map_grads[0:state, :]
    gc_ref[...] = map_grads[state : 2 * state, :]
    stores[4].start()
    stores[5].start()

    def end_tp(d, c):
        tp_copy(me_tp, lax.rem(me_tp + d, ntp)).wait_send()
        return c

    def end_tot(d, c):
        tot_copy(me, lax.rem(me + d, n)).wait_send()
        return c

    def end_states(d, c):
        level_copy(me, lax.rem(me + 2 * d, n), 0).wait_send()
        return c

    def end_kv(at, c):
        kv_copy(me, 2 * at + column).wait_send()
        return c

    def end_kv_forward(at, c):
        kv_forward(2 * at + column).wait_send()
        return c

    def end_grads(dst, c):
        grad_copy(me, dst).wait_send()
        return c

    lax.fori_loop(1, ntp, end_tp, 0)
    lax.fori_loop(1, n, end_tot, 0)
    pair_copy().wait_send()
    back_copy().wait_send()
    lax.fori_loop(1, levels, end_states, 0)

    @pl.when(column == 0)
    def _():
        kv_copy(me, partner).wait_send()

    lax.fori_loop(level + 1, levels, end_kv, 0)
    lax.fori_loop(0, level, end_kv_forward, 0)
    lax.fori_loop(0, me, end_grads, 0)
    for store in stores:
        store.wait()


def write_out(*refs):
    count = len(refs) // 3
    ins, outs, held = refs[:count], refs[count : 2 * count], refs[2 * count : 3 * count]
    sems = refs[-1]
    arrive = [pltpu.make_async_copy(ins[at], held[at], sems.at[0, at]) for at in range(count)]
    leave = [pltpu.make_async_copy(held[at], outs[at], sems.at[1, at]) for at in range(count)]
    for copy in arrive:
        copy.start()
    for at in range(count):
        arrive[at].wait()
        leave[at].start()
    for copy in leave:
        copy.wait()


def local(
    n,
    ntp,
    queries,
    key_vectors,
    value_vectors,
    attention_out,
    grad_attention,
    mix_input,
    grad_mix,
    input_map,
    output_map,
    decay_log,
):
    tokens, heads, width = queries.shape
    channels = mix_input.shape[1]
    state = input_map.shape[1]
    groups = decay_log.shape[1]
    rows = tokens * heads
    flat = lambda a: a.reshape(-1, width)
    hbm = pl.BlockSpec(memory_space=pltpu.HBM)
    dma = pltpu.SemaphoreType.DMA
    shapes = (
        jax.ShapeDtypeStruct((rows, width), BF16),
        jax.ShapeDtypeStruct((tokens, width), BF16),
        jax.ShapeDtypeStruct((tokens, width), BF16),
        jax.ShapeDtypeStruct((tokens, channels), BF16),
        jax.ShapeDtypeStruct((state, tokens), F32),
        jax.ShapeDtypeStruct((state, tokens), F32),
        jax.ShapeDtypeStruct((groups, tokens), F32),
    )
    outs = pl.pallas_call(
        functools.partial(kernel, n, ntp, heads),
        out_shape=shapes,
        in_specs=[hbm] * 10,
        out_specs=(hbm,) * 7,
        scratch_shapes=[pltpu.VMEM(out.shape, out.dtype) for out in shapes]
        + [
            pltpu.VMEM((rows, width), BF16),
            pltpu.VMEM((rows, width), BF16),
            pltpu.VMEM((rows, width), BF16),
            pltpu.VMEM((tokens, channels), BF16),
            pltpu.VMEM((tokens, channels), BF16),
            pltpu.VMEM((state, tokens), F32),
            pltpu.VMEM((state, tokens), F32),
            pltpu.VMEM((groups, tokens), F32),
            pltpu.VMEM((n, 2 * tokens, width), BF16),
            pltpu.VMEM((2, 2, state, channels // 2), F32),
            pltpu.VMEM((2, state, channels // 2), F32),
            pltpu.VMEM((2, state, channels // 2), BF16),
            pltpu.VMEM((n // 2, state, channels // 2), BF16),
            pltpu.VMEM((2, state, channels // 2), F32),
            pltpu.VMEM((2, state, channels // 2), F32),
            pltpu.VMEM((2, state, channels // 2), F32),
            pltpu.VMEM((2, state, channels // 2), F32),
            pltpu.VMEM((n, 8, 128), F32),
            pltpu.VMEM((n, 2 * tokens, width), BF16),
            pltpu.VMEM((n, 2 * tokens, width), BF16),
            pltpu.VMEM((n // 2, 2 * tokens, width), BF16),
            pltpu.VMEM((n // 2, 2 * tokens, width), F32),
            pltpu.VMEM((ntp, 2 * state, tokens), F32),
            pltpu.VMEM((tokens + 2 * state, channels), BF16),
            pltpu.VMEM((tokens + 2 * state, channels), BF16),
            pltpu.VMEM((state, channels), F32),
            pltpu.VMEM((tokens, channels), F32),
            pltpu.VMEM((tokens, channels), F32),
            pltpu.VMEM((state, channels), F32),
            pltpu.VMEM((n // 2, channels // 2), F32),
            pltpu.VMEM((tokens, channels), F32),
            pltpu.VMEM((tokens, channels), F32),
            pltpu.VMEM((2 * state, tokens), F32),
            pltpu.VMEM((8, rows), F32),
            pltpu.VMEM((8, rows), F32),
            pltpu.VMEM((8, rows), F32),
            pltpu.VMEM((width, rows), F32),
            dma((10,)),
            dma((7,)),
            dma((n,)),
            dma((n,)),
            dma((n,)),
            dma((n,)),
            dma((n,)),
            dma((n,)),
            dma((n,)),
            dma((n,)),
            dma((n,)),
            dma((n,)),
            dma((n // 2,)),
            dma((ntp,)),
            dma((ntp,)),
        ],
        compiler_params=pltpu.CompilerParams(
            collective_id=0, has_side_effects=True, vmem_limit_bytes=63 * 1024 * 1024
        ),
        name="layer_grads",
    )(
        flat(queries),
        flat(key_vectors),
        flat(value_vectors),
        flat(attention_out),
        flat(grad_attention),
        mix_input,
        grad_mix,
        input_map.T,
        output_map.T,
        decay_log.T,
    )
    outs = pl.pallas_call(
        write_out,
        out_shape=shapes,
        in_specs=[hbm] * 7,
        out_specs=(hbm,) * 7,
        compiler_params=pltpu.CompilerParams(vmem_limit_bytes=63 * 1024 * 1024),
        scratch_shapes=[pltpu.VMEM(out.shape, out.dtype) for out in shapes] + [dma((2, 7))],
        name="write_out",
    )(*outs)
    return (
        outs[0].reshape(queries.shape),
        outs[1].reshape(key_vectors.shape),
        outs[2].reshape(value_vectors.shape),
        outs[3], outs[4].T, outs[5].T, outs[6].T)


def solution(mesh):
    seq = P("ctx", "tp", None)
    both = P("ctx", "tp")
    ctx = P("ctx", None)
    return jax.shard_map(
        functools.partial(local, mesh.shape["ctx"], mesh.shape["tp"]),
        mesh=mesh,
        in_specs=(seq, seq, seq, seq, seq, both, both, ctx, ctx, both),
        out_specs=(seq, seq, seq, both, ctx, ctx, both),
        check_vma=False,
    )
```
